256 devices in a mesh: face: 2 (over core), tile: 128 (over x, z, y).
Axes of the slice: x: 4, y: 4, z: 8, core: 2. Of those that a mesh axis runs over, the one named last changes fastest.
Arguments:
- fwd_tracers: bfloat16 [2, 90, 4, 32768], P(None, None, None, ('face', 'tile')), may hold values from -6 to 6
- fwd_kappa: bfloat16 [90, 4, 32768], P(None, None, ('face', 'tile')), may hold values from 0.049804688 to 2
- send_order: int32 [2, 128, 128], P('face', 'tile'), may hold values from 0 to 127, each once within a row
- recv_place: int32 [2, 128, 128], P('face', 'tile'), may hold values from 0 to 127, each once within a row
- depth_levels: int32 [512, 256], P('tile', 'face'), may hold values from 0 to 90
- horiz_rate: float32 [90], replicated, may hold values from 0.03 to 0.24
- adj_init: float32 [2, 90, 512, 256], P(None, None, 'tile', 'face'), may hold values from -6 to 6
- misfit: float32 [2, 90, 512, 256], P(None, None, 'tile', 'face'), may hold values from -4 to 4
- ctrl_send: int32 [2, 128, 128], P('face', 'tile'), may hold values from 0 to 127, each once within a row
- ctrl_place: int32 [2, 128, 128], P('face', 'tile'), may hold values from 0 to 127, each once within a row
Outputs:
- sensitivity: float32 [2, 90, 4, 32768], P(None, None, None, ('face', 'tile'))
The draws below stay inside these ranges and needn't reach their ends.
Inputs may be any that keep to these rules, and one draw needn't show every extreme that they name: `send_order`: each row (last dimension) lists every number of 0 to 127 once. `recv_place`: each row (last dimension) lists every number of 0 to 127 once. `ctrl_send`: each row (last dimension) lists every number of 0 to 127 once. `ctrl_place`: each row (last dimension) lists every number of 0 to 127 once.
All inputs are finite; a program needn't handle non-finite values.
Results may differ from the reference program's by a relative error of at most 0.00095.
Values may be sent and summed in bfloat16 or wider, within the bound.
A program may use at most 64 MiB of HBM per device.

```python
import math
import jax
import jax.numpy as jnp
from jax import lax

LEV = 90
CX = 4
PY = 1
STEPS = 5
TILES = 128
FACES = 2
NX = 512
NY = 128
SLOTS = 32768


def draw_depth_levels(key, part):
    key = jax.random.fold_in(key, 7)
    first_key, second_key = jax.random.split(key)
    base = jax.random.randint(first_key, (NX, 2 * NY), -LEV, LEV + 1)
    offsets = jax.random.randint(second_key, (NX // CX, 1), 0, LEV + 1)
    offsets = jnp.repeat(offsets, CX, axis=0)
    return jnp.clip(base + offsets, 0, LEV).astype(jnp.int32)


def level_of(own_key, shape, cuts, low, largest):
    def one(dim, shards_of):
        draws = jax.random.uniform(jax.random.fold_in(jax.random.fold_in(own_key, 6), dim), (shards_of,), jnp.float32, low / len(cuts), largest / len(cuts))
        return jnp.repeat(jnp.exp(draws), shape[dim] // shards_of).reshape((-1,) + (1,) * (len(shape) - dim - 1))

    level = one(*cuts[0])
    for cut in cuts[1:]:
        level = level * one(*cut)
    return level


def normal_values(key, shape, width, most, cuts=(), kind=jnp.bfloat16):
    values = jax.random.normal(key, shape, jnp.float32) * width
    if len(cuts) > 0:
        values = level_of(key, shape, cuts, -0.22, 0.18) * values
    return jnp.clip(values, min=-most, max=most).astype(kind)


def setup_inputs(seed: int = 0) -> dict:
    keys = jax.random.split(jax.random.key(seed), 11)
    return {
        "fwd_tracers": normal_values(keys[0], (2, LEV, CX, SLOTS), 1.0, 6.0, ((3, 256),)),
        "fwd_kappa": jnp.clip(jnp.exp(math.log(2.0) - 3.6927934 * jax.random.uniform(keys[1], (LEV, CX, SLOTS), jnp.float32) ** level_of(keys[1], (LEV, CX, SLOTS), ((2, 256),), -0.2, 0.2)), 0.049804688, 2.0).astype(jnp.bfloat16),
        "send_order": jax.vmap(lambda own: jax.random.permutation(own, TILES))(jax.random.split(keys[2], FACES * TILES)).reshape((FACES, TILES, TILES)).astype(jnp.int32),
        "recv_place": jax.vmap(lambda own: jax.random.permutation(own, TILES))(jax.random.split(keys[3], FACES * TILES)).reshape((FACES, TILES, TILES)).astype(jnp.int32),
        "depth_levels": draw_depth_levels(jax.random.fold_in(keys[10], 71), 0),
        "horiz_rate": jnp.clip(jnp.exp(jax.random.uniform(keys[5], (LEV,), jnp.float32, math.log(0.03), math.log(0.24))), 0.03, 0.24),
        "adj_init": normal_values(keys[6], (2, LEV, NX, FACES * NY), 1.0, 6.0, ((2, 128), (3, 2)), jnp.float32),
        "misfit": normal_values(keys[7], (2, LEV, NX, FACES * NY), 0.5, 4.0, ((2, 128), (3, 2)), jnp.float32),
        "ctrl_send": jax.vmap(lambda own: jax.random.permutation(own, TILES))(jax.random.split(keys[8], FACES * TILES)).reshape((FACES, TILES, TILES)).astype(jnp.int32),
        "ctrl_place": jax.vmap(lambda own: jax.random.permutation(own, TILES))(jax.random.split(keys[9], FACES * TILES)).reshape((FACES, TILES, TILES)).astype(jnp.int32),
    }


def make_coupling(temper, salinity, kappa):
    temper = temper.astype(jnp.float32)
    salinity = salinity.astype(jnp.float32)
    kappa = kappa.astype(jnp.float32)
    density = 0.8 * salinity - 0.2 * temper
    contrast = density[1:] - density[:-1]
    inner = 0.5 * (kappa[:-1] + kappa[1:]) * (1.0 + 3.0 * jax.nn.sigmoid(-4.0 * contrast))
    bottom = jnp.zeros_like(inner[:1])
    return jnp.concatenate([inner, bottom], axis=0).astype(jnp.bfloat16)

def to_home(stored, send_order, recv_place):
    count = stored.shape[0]
    faces = send_order.shape[0]
    tiles = send_order.shape[1]
    grid = stored.reshape(count, LEV, CX, faces, tiles, tiles, PY)
    grid = jnp.transpose(grid, (0, 1, 2, 6, 3, 4, 5))
    face_index = jnp.arange(faces, dtype=jnp.int32)[:, None, None]
    tile_index = jnp.arange(tiles, dtype=jnp.int32)[None, :, None]
    picked = grid[..., face_index, tile_index, send_order]
    inverse = jnp.argsort(recv_place, axis=-1).astype(jnp.int32)
    placed = picked[..., face_index, inverse, tile_index]
    placed = jnp.transpose(placed, (0, 1, 5, 2, 4, 6, 3))
    return placed.reshape(count, LEV, tiles * CX, faces * tiles * PY)

def to_control(adjoint, ctrl_send, ctrl_place):
    count = adjoint.shape[0]
    faces = ctrl_send.shape[0]
    tiles = ctrl_send.shape[1]
    grid = adjoint.reshape(count, LEV, tiles, CX, faces, tiles, PY)
    grid = jnp.transpose(grid, (0, 1, 3, 6, 4, 2, 5))
    face_index = jnp.arange(faces, dtype=jnp.int32)[:, None, None]
    tile_index = jnp.arange(tiles, dtype=jnp.int32)[None, :, None]
    picked = grid[..., face_index, tile_index, ctrl_send]
    inverse = jnp.argsort(ctrl_place, axis=-1).astype(jnp.int32)
    placed = picked[..., face_index, inverse, tile_index]
    placed = jnp.transpose(placed, (0, 1, 2, 4, 5, 6, 3))
    return placed.reshape(count, LEV, CX, faces * tiles * tiles * PY)

def reference(fwd_tracers, fwd_kappa, send_order, recv_place, depth_levels, horiz_rate, adj_init, misfit, ctrl_send, ctrl_place):
    home_tracers = to_home(fwd_tracers, send_order, recv_place)
    home_kappa = to_home(fwd_kappa[None], send_order, recv_place)[0]
    coupling = make_coupling(home_tracers[0], home_tracers[1], home_kappa).astype(jnp.float32)
    levels = jnp.arange(LEV, dtype=jnp.int32)[:, None, None]
    wet_mask = (levels < depth_levels[None]).astype(jnp.float32)
    below = jnp.concatenate([wet_mask[1:], jnp.zeros_like(wet_mask[:1])], axis=0)
    weight = coupling * wet_mask * below
    above = jnp.concatenate([jnp.zeros_like(weight[:1]), weight[:-1]], axis=0)
    diagonal = 1.0 + weight + above
    padded_wet = jnp.pad(wet_mask, ((0, 0), (1, 1), (1, 1)))
    east = wet_mask * padded_wet[:, 2:, 1:-1]
    west = wet_mask * padded_wet[:, :-2, 1:-1]
    north = wet_mask * padded_wet[:, 1:-1, 2:]
    south = wet_mask * padded_wet[:, 1:-1, :-2]
    rate = horiz_rate[:, None, None]
    lower_band = jnp.moveaxis(-above, 0, -1)
    main_band = jnp.moveaxis(diagonal, 0, -1)
    upper_band = jnp.moveaxis(-weight, 0, -1)
    adjoint = adj_init
    for step_index in range(STEPS):
        padded = jnp.pad(adjoint, ((0, 0), (0, 0), (1, 1), (1, 1)))
        flux = east * (padded[:, :, 2:, 1:-1] - adjoint)
        flux = flux + west * (padded[:, :, :-2, 1:-1] - adjoint)
        flux = flux + north * (padded[:, :, 1:-1, 2:] - adjoint)
        flux = flux + south * (padded[:, :, 1:-1, :-2] - adjoint)
        spread = adjoint + rate * flux
        right_side = jnp.moveaxis(spread, (0, 1), (3, 2))
        solved = lax.linalg.tridiagonal_solve(lower_band, main_band, upper_band, right_side)
        solved = jnp.moveaxis(solved, (3, 2), (0, 1))
        adjoint = wet_mask * solved + wet_mask * misfit
    return to_control(adjoint, ctrl_send, ctrl_place)
```

```python
import functools

import jax
import jax.numpy as jnp
from jax import lax
from jax.experimental import pallas as pl
from jax.experimental.pallas import tpu as pltpu
from jax.sharding import PartitionSpec as P

MESH = pl.DeviceIdType.MESH
F32 = jnp.float32
BF16 = jnp.bfloat16
I32 = jnp.int32

LEV = 90
STEPS = 5
LANES = 128
UNROLL = 10
SIDES = ((0, 1), (1, -1))


def ordered(slot, face0, face1):
    return (face0, face1) if slot % 2 == 0 else (face1, face0)


def stack_faces(slot, face0, face1):
    first, second = ordered(slot, face0, face1)
    return jnp.concatenate([first, second], axis=0)


def in_slot(index_array):
    rows = lax.broadcasted_iota(I32, (LANES, LANES), 0)
    return (rows == index_array).astype(F32)


def column_dot(lhs, rhs):
    return lax.dot_general(lhs, rhs, (((1,), (1,)), ((), ())), preferred_element_type=F32)


def row_dot(lhs, rhs):
    return lax.dot_general(lhs, rhs, (((0,), (1,)), ((), ())), preferred_element_type=F32)


def kernel(
    tiles,
    fwd, kap, send_order, recv_place, depth, rate, adj, mis, ctrl_send, ctrl_place,
    out,
    fwd_v, kap_v, so_v, rp_v, depth_v, adj_v, mis_v, cs_v, cp_v,
    coup_v, stage, send_one, land_one,
    meta, metas, half_adj, half_mis, edge_adj, halo_adj, halo_mis, halo_edge, own_adj, own_mis,
    placed, state, middle, keep, factor, inverse, source,
    final, other, send_two, land_two, stage_two,
    local, meta_sem, one_sem, pass_sem, halo_sem, pair_sem, two_sem,
):
    tile = lax.axis_index("tile")
    face = lax.axis_index("face")
    barrier = pltpu.get_barrier_semaphore()

    def to_tile(shift):
        return lax.rem(tile + (shift + tiles), tiles)

    def greet(step, carry):
        pl.semaphore_signal(
            barrier, inc=1, device_id=(face, lax.rem(tile + step, tiles)), device_id_type=MESH
        )
        return carry

    for shift in (-2, -1, 0, 1, 2):
        pl.semaphore_signal(
            barrier, inc=1, device_id=(1 - face, to_tile(shift)), device_id_type=MESH
        )
    lax.fori_loop(1, tiles, greet, 0)

    moves = [
        pltpu.make_async_copy(src, dst, local.at[i])
        for i, (src, dst) in enumerate((
            (fwd, fwd_v.at[:, pl.ds(0, LEV)]),
            (kap, kap_v.at[pl.ds(0, LEV)]),
            (send_order.at[0], so_v),
            (recv_place.at[0], rp_v),
            (depth, depth_v),
            (adj, adj_v),
            (mis, mis_v),
            (ctrl_send.at[0], cs_v),
            (ctrl_place.at[0], cp_v),
            (adj.at[face], own_adj.at[face]),
            (mis.at[face], own_mis.at[face]),
        ))
    ]
    for move in moves:
        move.start()
    fwd_v[0, LEV] = jnp.zeros((4, LANES), BF16)
    fwd_v[1, LEV] = jnp.zeros((4, LANES), BF16)
    kap_v[LEV] = jnp.zeros((4, LANES), BF16)
    coup_v[pl.ds(4 * LEV, 24)] = jnp.zeros((24, LANES), F32)
    stage[:, 3, :] = jnp.zeros((LANES, LANES), F32)

    for move in moves[:4]:
        move.wait()

    def density(level):
        return 0.8 * fwd_v[1, level].astype(F32) - 0.2 * fwd_v[0, level].astype(F32)

    def couple(block, carry):
        above, kappa_above = carry
        for pair in range(5):
            rows = []
            for half in range(2):
                level = block * 10 + pair * 2 + half + 1
                below = density(level)
                kappa_below = kap_v[level].astype(F32)
                contrast = below - above
                rows.append(
                    0.5 * (kappa_above + kappa_below) * (1.0 + 3.0 * jax.nn.sigmoid(-4.0 * contrast))
                )
                above, kappa_above = below, kappa_below
            coup_v[pl.ds(pl.multiple_of(block * 40 + pair * 8, 8), 8)] = jnp.concatenate(rows, axis=0)
        return above, kappa_above

    lax.fori_loop(0, LEV // 10, couple, (density(0), kap_v[0].astype(F32)))

    pick = in_slot(so_v[...]).T.astype(BF16)
    pieces = column_dot(pick, coup_v[...].astype(BF16))
    for part in range(3):
        stage[:, part, :] = pieces[:, part * LANES : (part + 1) * LANES]
    packed = stage[...].astype(BF16)
    send_one[pl.ds(1, tiles)] = packed
    send_one[0] = packed[tiles - 1]
    send_one[tiles + 1] = packed[0]

    moves[4].wait()
    meta[0] = jnp.concatenate([depth_v[...], depth_v[...]], axis=0)
    meta[1] = jnp.broadcast_to(rp_v[...], (8, LANES))
    metas[4 + face] = meta[...]
    moves[5].wait()
    for tracer in range(2):
        half_adj[tracer] = adj_v[tracer].astype(BF16)
        edge_adj[0, tracer] = adj_v[tracer, :, 3:4, :]
        edge_adj[1, tracer] = adj_v[tracer, :, 0:1, :]
    moves[6].wait()
    for tracer in range(2):
        half_mis[tracer] = mis_v[tracer].astype(BF16)

    pl.semaphore_wait(barrier, tiles + 4)

    def remote(src, dst, send_sem, recv_sem, to_face, to):
        pltpu.make_async_remote_copy(
            src_ref=src, dst_ref=dst, send_sem=send_sem, recv_sem=recv_sem,
            device_id=(to_face, to), device_id_type=MESH,
        ).start()

    for shift in (-1, 1, -2, 2):
        for tracer in range(2):
            remote(
                meta, metas.at[2 * (2 - shift) + face],
                meta_sem.at[0], meta_sem.at[1], tracer, to_tile(shift),
            )
    remote(meta, metas.at[4 + face], meta_sem.at[0], meta_sem.at[1], 1 - face, tile)
    remote(
        adj.at[1 - face], own_adj.at[face], pair_sem.at[0], pair_sem.at[1], 1 - face, tile
    )
    remote(
        mis.at[1 - face], own_mis.at[face], pair_sem.at[2], pair_sem.at[3], 1 - face, tile
    )

    def route_one(step, carry):
        to = lax.rem(tile + step, tiles)
        remote(
            send_one.at[pl.ds(to, 3)], land_one.at[0, tile], one_sem.at[0], one_sem.at[1], face, to
        )
        return carry

    lax.fori_loop(1, tiles, route_one, 0)
    self_one = pltpu.make_async_copy(
        send_one.at[pl.ds(tile, 3)], land_one.at[0, tile], local.at[11]
    )
    self_one.start()
    for side, shift in SIDES:
        for tracer in range(2):
            remote(
                half_adj.at[tracer], halo_adj.at[2 * side + face],
                halo_sem.at[0], halo_sem.at[1], tracer, to_tile(shift),
            )
            remote(
                edge_adj.at[side, tracer], halo_edge.at[2 * side + face],
                halo_sem.at[2], halo_sem.at[3], tracer, to_tile(2 * shift),
            )
    for side, shift in SIDES:
        for tracer in range(2):
            remote(
                half_mis.at[tracer], halo_mis.at[2 * side + face],
                halo_sem.at[4], halo_sem.at[5], tracer, to_tile(shift),
            )

    def arrived(ref, semaphore):
        pltpu.make_async_copy(ref, ref, semaphore).wait()

    row = lax.broadcasted_iota(I32, (8, LANES), 0)
    lane = lax.broadcasted_iota(I32, (8, LANES), 1)
    cell = row % 4
    first_cell, last_cell = cell == 0, cell == 3
    first_lane, last_lane = lane == 0, lane == LANES - 1
    low_lane, low_row = lane < LANES // 2, row < 4
    seam_even = low_lane == low_row
    seam_odd = low_lane != low_row

    def neighbours(slot, west, here, east):
        seam = jnp.where(seam_even if slot % 2 == 0 else seam_odd, pltpu.roll(here, 4, 0), 0.0)
        return (
            pltpu.roll(jnp.where(first_cell, east, here), 7, 0),
            pltpu.roll(jnp.where(last_cell, west, here), 1, 0),
            pltpu.roll(jnp.where(first_lane, seam, here), LANES - 1, 1),
            pltpu.roll(jnp.where(last_lane, seam, here), 1, 1),
        )

    arrived(metas.at[pl.ds(0, 9)], meta_sem.at[1])
    depths = []
    for slot in range(5):
        at = tile + (slot - 2)
        inside = jnp.logical_and(at >= 0, at < tiles).astype(F32)
        first, second = ordered(slot, metas[2 * slot, 0], metas[2 * slot + 1, 0])
        depths.append(jnp.where(low_row, first, second).astype(F32) * inside)
    around = [
        neighbours(slot, depths[slot - 1], depths[slot], depths[slot + 1]) for slot in (1, 2, 3)
    ]

    def wet(level, slot):
        return level.astype(F32) < depths[slot]

    def prepare(block, carry):
        for inner in range(5):
            level = block * 5 + inner
            at = level.astype(F32)
            speed = rate[level]
            for slot in (1, 2, 3):
                count = jnp.zeros((8, LANES), F32)
                for beside in around[slot - 1]:
                    count = count + jnp.where(at < beside, 1.0, 0.0)
                keep[level, slot - 1] = 1.0 - speed * count
        return carry

    lax.fori_loop(0, LEV // 5, prepare, 0)

    moves[9].wait()
    arrived(own_adj.at[0], pair_sem.at[1])
    arrived(halo_adj, halo_sem.at[1])
    arrived(halo_edge, halo_sem.at[3])

    def begin(block, carry):
        for inner in range(5):
            level = block * 5 + inner
            tile_of = {
                1: stack_faces(1, halo_adj[0, level].astype(F32), halo_adj[1, level].astype(F32)),
                2: stack_faces(2, own_adj[0, level], own_adj[1, level]),
                3: stack_faces(3, halo_adj[2, level].astype(F32), halo_adj[3, level].astype(F32)),
                0: jnp.where(low_row, halo_edge[0, level], halo_edge[1, level]),
                4: jnp.where(low_row, halo_edge[2, level], halo_edge[3, level]),
            }
            for slot in range(5):
                state[level, slot] = jnp.where(wet(level, slot), tile_of[slot], 0.0)
        return carry

    lax.fori_loop(0, LEV // 5, begin, 0)

    moves[10].wait()
    arrived(own_mis.at[0], pair_sem.at[3])
    arrived(halo_mis, halo_sem.at[5])

    def drive(block, carry):
        for inner in range(5):
            level = block * 5 + inner
            tile_of = {
                1: stack_faces(1, halo_mis[0, level].astype(F32), halo_mis[1, level].astype(F32)),
                2: stack_faces(2, own_mis[0, level], own_mis[1, level]),
                3: stack_faces(3, halo_mis[2, level].astype(F32), halo_mis[3, level].astype(F32)),
            }
            for slot in (1, 2, 3):
                source[level, slot - 1] = jnp.where(wet(level, slot), tile_of[slot], 0.0)
        return carry

    lax.fori_loop(0, LEV // 5, drive, 0)

    self_one.wait()
    arrived(land_one.at[0, pl.ds(0, tiles - 1)], one_sem.at[1])
    remote(land_one.at[0], land_one.at[1], pass_sem.at[0], pass_sem.at[1], 1 - face, tile)
    for source_of in range(2):
        if source_of == 1:
            arrived(land_one.at[1], pass_sem.at[1])
        which = face if source_of == 0 else 1 - face
        for part in range(3):
            stage[...] = land_one[source_of, :, part].astype(F32)
            held = jnp.concatenate([stage[:, i, :] for i in range(3)], axis=1).astype(BF16)
            place = in_slot(metas[2 * (part + 1) + which, 1][0:1, :]).astype(BF16)
            placed[which, part] = row_dot(held, place)

    one = jnp.ones((8, LANES), F32)

    def eliminate(block, carry):
        carry = [(upper / lower, one) for upper, lower in carry]
        for pair in range(UNROLL // 2):
            base = pl.multiple_of(block * (4 * UNROLL) + pair * 8, 8)
            for slot in (1, 2, 3):
                first, second = ordered(
                    slot, placed[0, slot - 1, pl.ds(base, 8)], placed[1, slot - 1, pl.ds(base, 8)]
                )
                couplings = (
                    jnp.where(low_row, first, pltpu.roll(second, 4, 0)),
                    jnp.where(low_row, pltpu.roll(first, 4, 0), second),
                )
                upper, lower = carry[slot - 1]
                for half in range(2):
                    level = block * UNROLL + pair * 2 + half
                    weight = jnp.where(
                        (level + 1).astype(F32) < depths[slot], couplings[half], 0.0
                    )
                    next_lower = upper + weight * lower
                    next_upper = next_lower + weight * upper
                    ratio = lower / next_lower
                    factor[level, slot - 1] = weight * ratio
                    inverse[level, slot - 1] = jnp.where(wet(level, slot), ratio, 0.0)
                    upper, lower = next_upper, next_lower
                carry[slot - 1] = (upper, lower)
        return carry

    lax.fori_loop(0, LEV // UNROLL, eliminate, [(one, one)] * 3)

    zero = jnp.zeros((8, LANES), F32)

    def descend(slots, block, carry):
        carry = list(carry)
        for inner in range(UNROLL):
            level = block * UNROLL + inner
            speed = rate[level]
            tile_of = {
                slot: state[level, slot] for slot in range(slots[0] - 1, slots[-1] + 2)
            }
            for i, slot in enumerate(slots):
                east, west, north, south = neighbours(
                    slot, tile_of[slot - 1], tile_of[slot], tile_of[slot + 1]
                )
                spread = keep[level, slot - 1] * tile_of[slot] + speed * (
                    (east + west) + (north + south)
                )
                value = spread + carry[i]
                middle[level, slot - 1] = value
                carry[i] = factor[level, slot - 1] * value
        return carry

    def ascend(slots, last, block, carry):
        carry = list(carry)
        for pair in range(UNROLL // 2):
            halves = []
            for inner in range(2):
                level = (LEV - 1) - (block * UNROLL + pair * 2 + inner)
                for i, slot in enumerate(slots):
                    solved = (
                        middle[level, slot - 1] * inverse[level, slot - 1]
                        + factor[level, slot - 1] * carry[i]
                    )
                    carry[i] = solved
                    value = solved + source[level, slot - 1]
                    if last:
                        halves.append(value)
                    else:
                        state[level, slot] = value
            if last:
                below, above = halves
                base = pl.multiple_of(
                    (4 * LEV - 8) - (block * (4 * UNROLL) + pair * 8), 8
                )
                final[0, pl.ds(base, 8)] = jnp.where(low_row, above, pltpu.roll(below, 4, 0))
                final[1, pl.ds(base, 8)] = jnp.where(low_row, pltpu.roll(above, 4, 0), below)
        return carry

    def advance(step, carry):
        lax.fori_loop(0, LEV // UNROLL, functools.partial(descend, (1, 2, 3)), [zero] * 3)
        lax.fori_loop(0, LEV // UNROLL, functools.partial(ascend, (1, 2, 3), False), [zero] * 3)
        return carry

    lax.fori_loop(0, STEPS - 1, advance, 0)
    lax.fori_loop(0, LEV // UNROLL, functools.partial(descend, (2,)), [zero])
    final[0, pl.ds(4 * LEV, 24)] = jnp.zeros((24, LANES), F32)
    final[1, pl.ds(4 * LEV, 24)] = jnp.zeros((24, LANES), F32)
    lax.fori_loop(0, LEV // UNROLL, functools.partial(ascend, (2,), True), [zero])

    remote(final.at[1 - face], other, pair_sem.at[4], pair_sem.at[5], 1 - face, tile)
    moves[7].wait()
    moves[8].wait()
    choose = in_slot(cs_v[...]).T.astype(BF16)
    for source_of in range(2):
        if source_of == 0:
            values, tracer = final[face], face
        else:
            arrived(other, pair_sem.at[5])
            values, tracer = other[...], 1 - face
        high = values.astype(BF16)
        low = (values - high.astype(F32)).astype(BF16)
        pieces = column_dot(choose, high) + column_dot(choose, low)
        for part in range(3):
            stage_two[tracer, :, part, :] = pieces[:, part * LANES : (part + 1) * LANES]
    for part in range(6):
        send_two[:, part // 2, part % 2, :] = stage_two[part // 3, :, part % 3, :]

    def route_two(step, carry):
        to = lax.rem(tile + step, tiles)
        remote(send_two.at[to], land_two.at[tile], two_sem.at[0], two_sem.at[1], face, to)
        return carry

    lax.fori_loop(1, tiles, route_two, 0)
    self_two = pltpu.make_async_copy(send_two.at[tile], land_two.at[tile], local.at[12])
    self_two.start()
    place = in_slot(cp_v[...]).astype(BF16)
    self_two.wait()
    arrived(land_two.at[pl.ds(0, tiles - 1)], two_sem.at[1])
    for tracer in range(2):
        values = jnp.concatenate(
            [land_two[:, part // 2, part % 2, :] for part in range(3 * tracer, 3 * tracer + 3)],
            axis=1,
        )
        high = values.astype(BF16)
        low = (values - high.astype(F32)).astype(BF16)
        result = row_dot(high, place) + row_dot(low, place)
        out[tracer] = result[: 4 * LEV].reshape(LEV, 4, LANES)

    arrived(metas.at[pl.ds(0, 9)], meta_sem.at[0])
    arrived(own_adj.at[0], pair_sem.at[0])
    arrived(own_mis.at[0], pair_sem.at[2])
    arrived(land_one.at[0, pl.ds(0, tiles - 1)], one_sem.at[0])
    arrived(halo_adj, halo_sem.at[0])
    arrived(halo_edge, halo_sem.at[2])
    arrived(halo_mis, halo_sem.at[4])
    arrived(land_one.at[1], pass_sem.at[0])
    arrived(other, pair_sem.at[4])
    arrived(land_two.at[pl.ds(0, tiles - 1)], two_sem.at[0])


def per_device(
    fwd_tracers, fwd_kappa, send_order, recv_place, depth_levels, horiz_rate, adj_init, misfit,
    ctrl_send, ctrl_place,
):
    tiles = lax.axis_size("tile")
    anywhere = pl.BlockSpec(memory_space=pl.ANY)
    vmem = pltpu.VMEM
    dma = pltpu.SemaphoreType.DMA
    block = (LEV, 4, LANES)
    level_rows = (LEV, 3, 8, LANES)
    scratch = [
        vmem((2, LEV + 1, 4, LANES), BF16), vmem((LEV + 1, 4, LANES), BF16),
        vmem((1, LANES), I32), vmem((1, LANES), I32), vmem((4, LANES), I32),
        vmem((2,) + block, F32), vmem((2,) + block, F32),
        vmem((1, LANES), I32), vmem((1, LANES), I32),
        vmem((384, LANES), F32), vmem((tiles, 4, LANES), F32),
        vmem((tiles + 2, 4, LANES), BF16), vmem((2, tiles, 3, 4, LANES), BF16),
        vmem((2, 8, LANES), I32), vmem((10, 2, 8, LANES), I32),
        vmem((2,) + block, BF16), vmem((2,) + block, BF16), vmem((2, 2, LEV, 1, LANES), F32),
        vmem((4,) + block, BF16), vmem((4,) + block, BF16), vmem((4, LEV, 1, LANES), F32),
        vmem((2,) + block, F32), vmem((2,) + block, F32),
        vmem((2, 3, 384, LANES), F32), vmem((LEV, 5, 8, LANES), F32),
        vmem(level_rows, F32), vmem(level_rows, F32), vmem(level_rows, F32),
        vmem(level_rows, F32), vmem(level_rows, F32),
        vmem((2, 384, LANES), F32), vmem((384, LANES), F32),
        vmem((tiles, 3, 2, LANES), F32), vmem((tiles, 3, 2, LANES), F32),
        vmem((2, tiles, 3, LANES), F32),
        dma((13,)), dma((2,)), dma((2,)), dma((2,)), dma((6,)), dma((6,)), dma((2,)),
    ]
    return pl.pallas_call(
        functools.partial(kernel, tiles),
        out_shape=jax.ShapeDtypeStruct((2,) + block, F32),
        in_specs=[anywhere] * 5 + [pl.BlockSpec(memory_space=pltpu.SMEM)] + [anywhere] * 4,
        out_specs=pl.BlockSpec(memory_space=pltpu.VMEM),
        scratch_shapes=scratch,
        compiler_params=pltpu.CompilerParams(
            collective_id=0, has_side_effects=True, vmem_limit_bytes=48 * 2**20
        ),
        cost_estimate=pl.CostEstimate(
            flops=10**9, bytes_accessed=4 * 2**20, transcendentals=10**5
        ),
    )(
        fwd_tracers, fwd_kappa, send_order, recv_place, depth_levels, horiz_rate, adj_init, misfit,
        ctrl_send, ctrl_place,
    )


def solution(mesh):
    placed = (
        P(None, None, None, ("face", "tile")),
        P(None, None, ("face", "tile")),
        P("face", "tile", None),
        P("face", "tile", None),
        P("tile", "face"),
        P(),
        P(None, None, "tile", "face"),
        P(None, None, "tile", "face"),
        P("face", "tile", None),
        P("face", "tile", None),
    )
    return jax.shard_map(
        per_device,
        mesh=mesh,
        in_specs=placed,
        out_specs=P(None, None, None, ("face", "tile")),
        check_vma=False,
    )
```

```python
import functools

import jax
import jax.numpy as jnp
from jax import lax
from jax.experimental import pallas as pl
from jax.experimental.pallas import tpu as pltpu
from jax.sharding import PartitionSpec as P

MESH = pl.DeviceIdType.MESH
F32 = jnp.float32
BF16 = jnp.bfloat16
I32 = jnp.int32

LEV = 90
STEPS = 5
LANES = 128
UNROLL = 10
SIDES = ((0, 1), (1, -1))


def ordered(slot, face0, face1):
    return (face0, face1) if slot % 2 == 0 else (face1, face0)


def stack_faces(slot, face0, face1):
    first, second = ordered(slot, face0, face1)
    return jnp.concatenate([first, second], axis=0)


def in_slot(index_array):
    rows = lax.broadcasted_iota(I32, (LANES, LANES), 0)
    return (rows == index_array).astype(F32)


def column_dot(lhs, rhs):
    return lax.dot_general(lhs, rhs, (((1,), (1,)), ((), ())), preferred_element_type=F32)


def row_dot(lhs, rhs):
    return lax.dot_general(lhs, rhs, (((0,), (1,)), ((), ())), preferred_element_type=F32)


def kernel(
    tiles,
    fwd, kap, send_order, recv_place, depth, rate_in, adj, mis, ctrl_send, ctrl_place,
    out,
    rate, fwd_v, kap_v, so_v, rp_v, depth_v, adj_v, mis_v, cs_v, cp_v,
    coup_v, stage, send_one, land_one,
    meta, metas, half_adj, half_mis, edge_adj, halo_adj, halo_mis, halo_edge, own_adj, own_mis,
    placed, state, middle, keep, factor, inverse, source,
    final, other, send_two, land_two, stage_two,
    local, meta_sem, one_sem, pass_sem, halo_sem, pair_sem, two_sem,
):
    tile = lax.axis_index("tile")
    face = lax.axis_index("face")
    barrier = pltpu.get_barrier_semaphore()

    def to_tile(shift):
        return lax.rem(tile + (shift + tiles), tiles)

    def greet(step, carry):
        pl.semaphore_signal(
            barrier, inc=1, device_id=(face, lax.rem(tile + step, tiles)), device_id_type=MESH
        )
        return carry

    for shift in (-2, -1, 0, 1, 2):
        pl.semaphore_signal(
            barrier, inc=1, device_id=(1 - face, to_tile(shift)), device_id_type=MESH
        )
    lax.fori_loop(1, tiles, greet, 0)

    moves = [
        pltpu.make_async_copy(src, dst, local.at[i])
        for i, (src, dst) in enumerate((
            (fwd, fwd_v.at[:, pl.ds(0, LEV)]),
            (kap, kap_v.at[pl.ds(0, LEV)]),
            (send_order.at[0], so_v),
            (recv_place.at[0], rp_v),
            (depth, depth_v),
            (adj, adj_v),
            (mis, mis_v),
            (ctrl_send.at[0], cs_v),
            (ctrl_place.at[0], cp_v),
            (adj.at[face], own_adj.at[face]),
            (mis.at[face], own_mis.at[face]),
            (rate_in, rate),
        ))
    ]
    for move in moves:
        move.start()
    fwd_v[0, LEV] = jnp.zeros((4, LANES), BF16)
    fwd_v[1, LEV] = jnp.zeros((4, LANES), BF16)
    kap_v[LEV] = jnp.zeros((4, LANES), BF16)
    coup_v[pl.ds(4 * LEV, 24)] = jnp.zeros((24, LANES), F32)
    stage[:, 3, :] = jnp.zeros((LANES, LANES), F32)

    for move in moves[:4]:
        move.wait()

    def density(level):
        return 0.8 * fwd_v[1, level].astype(F32) - 0.2 * fwd_v[0, level].astype(F32)

    def couple(block, carry):
        above, kappa_above = carry
        for pair in range(5):
            rows = []
            for half in range(2):
                level = block * 10 + pair * 2 + half + 1
                below = density(level)
                kappa_below = kap_v[level].astype(F32)
                contrast = below - above
                rows.append(
                    0.5 * (kappa_above + kappa_below) * (1.0 + 3.0 * jax.nn.sigmoid(-4.0 * contrast))
                )
                above, kappa_above = below, kappa_below
            coup_v[pl.ds(pl.multiple_of(block * 40 + pair * 8, 8), 8)] = jnp.concatenate(rows, axis=0)
        return above, kappa_above

    lax.fori_loop(0, LEV // 10, couple, (density(0), kap_v[0].astype(F32)))

    pick = in_slot(so_v[...]).T.astype(BF16)
    pieces = column_dot(pick, coup_v[...].astype(BF16))
    for part in range(3):
        stage[:, part, :] = pieces[:, part * LANES : (part + 1) * LANES]
    packed = stage[...].astype(BF16)
    send_one[pl.ds(1, tiles)] = packed
    send_one[0] = packed[tiles - 1]
    send_one[tiles + 1] = packed[0]

    moves[4].wait()
    meta[0] = jnp.concatenate([depth_v[...], depth_v[...]], axis=0)
    meta[1] = jnp.broadcast_to(rp_v[...], (8, LANES))
    metas[4 + face] = meta[...]
    moves[5].wait()
    for tracer in range(2):
        half_adj[tracer] = adj_v[tracer].astype(BF16)
        edge_adj[0, tracer] = adj_v[tracer, :, 3:4, :]
        edge_adj[1, tracer] = adj_v[tracer, :, 0:1, :]
    moves[6].wait()
    for tracer in range(2):
        half_mis[tracer] = mis_v[tracer].astype(BF16)

    pl.semaphore_wait(barrier, tiles + 4)

    def remote(src, dst, send_sem, recv_sem, to_face, to):
        pltpu.make_async_remote_copy(
            src_ref=src, dst_ref=dst, send_sem=send_sem, recv_sem=recv_sem,
            device_id=(to_face, to), device_id_type=MESH,
        ).start()

    for shift in (-1, 1, -2, 2):
        for tracer in range(2):
            remote(
                meta, metas.at[2 * (2 - shift) + face],
                meta_sem.at[0], meta_sem.at[1], tracer, to_tile(shift),
            )
    remote(meta, metas.at[4 + face], meta_sem.at[0], meta_sem.at[1], 1 - face, tile)
    remote(
        adj.at[1 - face], own_adj.at[face], pair_sem.at[0], pair_sem.at[1], 1 - face, tile
    )
    remote(
        mis.at[1 - face], own_mis.at[face], pair_sem.at[2], pair_sem.at[3], 1 - face, tile
    )

    def route_one(step, carry):
        to = lax.rem(tile + step, tiles)
        remote(
            send_one.at[pl.ds(to, 3)], land_one.at[0, tile], one_sem.at[0], one_sem.at[1], face, to
        )
        return carry

    lax.fori_loop(1, tiles, route_one, 0)
    self_one = pltpu.make_async_copy(
        send_one.at[pl.ds(tile, 3)], land_one.at[0, tile], local.at[12]
    )
    self_one.start()
    for side, shift in SIDES:
        for tracer in range(2):
            remote(
                half_adj.at[tracer], halo_adj.at[2 * side + face],
                halo_sem.at[0], halo_sem.at[1], tracer, to_tile(shift),
            )
            remote(
                edge_adj.at[side, tracer], halo_edge.at[2 * side + face],
                halo_sem.at[2], halo_sem.at[3], tracer, to_tile(2 * shift),
            )
    for side, shift in SIDES:
        for tracer in range(2):
            remote(
                half_mis.at[tracer], halo_mis.at[2 * side + face],
                halo_sem.at[4], halo_sem.at[5], tracer, to_tile(shift),
            )

    def arrived(ref, semaphore):
        pltpu.make_async_copy(ref, ref, semaphore).wait()

    row = lax.broadcasted_iota(I32, (8, LANES), 0)
    lane = lax.broadcasted_iota(I32, (8, LANES), 1)
    cell = row % 4
    first_cell, last_cell = cell == 0, cell == 3
    first_lane, last_lane = lane == 0, lane == LANES - 1
    low_lane, low_row = lane < LANES // 2, row < 4
    seam_even = low_lane == low_row
    seam_odd = low_lane != low_row

    def neighbours(slot, west, here, east):
        seam = jnp.where(seam_even if slot % 2 == 0 else seam_odd, pltpu.roll(here, 4, 0), 0.0)
        return (
            pltpu.roll(jnp.where(first_cell, east, here), 7, 0),
            pltpu.roll(jnp.where(last_cell, west, here), 1, 0),
            pltpu.roll(jnp.where(first_lane, seam, here), LANES - 1, 1),
            pltpu.roll(jnp.where(last_lane, seam, here), 1, 1),
        )

    arrived(metas.at[pl.ds(0, 9)], meta_sem.at[1])
    depths = []
    for slot in range(5):
        at = tile + (slot - 2)
        inside = jnp.logical_and(at >= 0, at < tiles).astype(F32)
        first, second = ordered(slot, metas[2 * slot, 0], metas[2 * slot + 1, 0])
        depths.append(jnp.where(low_row, first, second).astype(F32) * inside)
    around = [
        neighbours(slot, depths[slot - 1], depths[slot], depths[slot + 1]) for slot in (1, 2, 3)
    ]

    def wet(level, slot):
        return level.astype(F32) < depths[slot]

    def prepare(block, carry):
        for inner in range(5):
            level = block * 5 + inner
            at = level.astype(F32)
            speed = rate[level]
            for slot in (1, 2, 3):
                count = jnp.zeros((8, LANES), F32)
                for beside in around[slot - 1]:
                    count = count + jnp.where(at < beside, 1.0, 0.0)
                keep[level, slot - 1] = 1.0 - speed * count
        return carry

    moves[11].wait()
    lax.fori_loop(0, LEV // 5, prepare, 0)

    moves[9].wait()
    arrived(own_adj.at[0], pair_sem.at[1])
    arrived(halo_adj, halo_sem.at[1])
    arrived(halo_edge, halo_sem.at[3])

    def begin(block, carry):
        for inner in range(5):
            level = block * 5 + inner
            tile_of = {
                1: stack_faces(1, halo_adj[0, level].astype(F32), halo_adj[1, level].astype(F32)),
                2: stack_faces(2, own_adj[0, level], own_adj[1, level]),
                3: stack_faces(3, halo_adj[2, level].astype(F32), halo_adj[3, level].astype(F32)),
                0: jnp.where(low_row, halo_edge[0, level], halo_edge[1, level]),
                4: jnp.where(low_row, halo_edge[2, level], halo_edge[3, level]),
            }
            for slot in range(5):
                state[level, slot] = jnp.where(wet(level, slot), tile_of[slot], 0.0)
        return carry

    lax.fori_loop(0, LEV // 5, begin, 0)

    moves[10].wait()
    arrived(own_mis.at[0], pair_sem.at[3])
    arrived(halo_mis, halo_sem.at[5])

    def drive(block, carry):
        for inner in range(5):
            level = block * 5 + inner
            tile_of = {
                1: stack_faces(1, halo_mis[0, level].astype(F32), halo_mis[1, level].astype(F32)),
                2: stack_faces(2, own_mis[0, level], own_mis[1, level]),
                3: stack_faces(3, halo_mis[2, level].astype(F32), halo_mis[3, level].astype(F32)),
            }
            for slot in (1, 2, 3):
                source[level, slot - 1] = jnp.where(wet(level, slot), tile_of[slot], 0.0)
        return carry

    lax.fori_loop(0, LEV // 5, drive, 0)

    self_one.wait()
    arrived(land_one.at[0, pl.ds(0, tiles - 1)], one_sem.at[1])
    remote(land_one.at[0], land_one.at[1], pass_sem.at[0], pass_sem.at[1], 1 - face, tile)
    for source_of in range(2):
        if source_of == 1:
            arrived(land_one.at[1], pass_sem.at[1])
        which = face if source_of == 0 else 1 - face
        for part in range(3):
            stage[...] = land_one[source_of, :, part].astype(F32)
            held = jnp.concatenate([stage[:, i, :] for i in range(3)], axis=1).astype(BF16)
            place = in_slot(metas[2 * (part + 1) + which, 1][0:1, :]).astype(BF16)
            placed[which, part] = row_dot(held, place)

    one = jnp.ones((8, LANES), F32)

    def eliminate(block, carry):
        carry = [(upper / lower, one) for upper, lower in carry]
        for pair in range(UNROLL // 2):
            base = pl.multiple_of(block * (4 * UNROLL) + pair * 8, 8)
            for slot in (1, 2, 3):
                first, second = ordered(
                    slot, placed[0, slot - 1, pl.ds(base, 8)], placed[1, slot - 1, pl.ds(base, 8)]
                )
                couplings = (
                    jnp.where(low_row, first, pltpu.roll(second, 4, 0)),
                    jnp.where(low_row, pltpu.roll(first, 4, 0), second),
                )
                upper, lower = carry[slot - 1]
                for half in range(2):
                    level = block * UNROLL + pair * 2 + half
                    weight = jnp.where(
                        (level + 1).astype(F32) < depths[slot], couplings[half], 0.0
                    )
                    next_lower = upper + weight * lower
                    next_upper = next_lower + weight * upper
                    ratio = lower / next_lower
                    factor[level, slot - 1] = weight * ratio
                    inverse[level, slot - 1] = jnp.where(wet(level, slot), ratio, 0.0)
                    upper, lower = next_upper, next_lower
                carry[slot - 1] = (upper, lower)
        return carry

    lax.fori_loop(0, LEV // UNROLL, eliminate, [(one, one)] * 3)

    zero = jnp.zeros((8, LANES), F32)

    def descend(slots, block, carry):
        carry = list(carry)
        for inner in range(UNROLL):
            level = block * UNROLL + inner
            speed = rate[level]
            tile_of = {
                slot: state[level, slot] for slot in range(slots[0] - 1, slots[-1] + 2)
            }
            for i, slot in enumerate(slots):
                east, west, north, south = neighbours(
                    slot, tile_of[slot - 1], tile_of[slot], tile_of[slot + 1]
                )
                spread = keep[level, slot - 1] * tile_of[slot] + speed * (
                    (east + west) + (north + south)
                )
                value = spread + carry[i]
                middle[level, slot - 1] = value
                carry[i] = factor[level, slot - 1] * value
        return carry

    def ascend(slots, last, block, carry):
        carry = list(carry)
        for pair in range(UNROLL // 2):
            halves = []
            for inner in range(2):
                level = (LEV - 1) - (block * UNROLL + pair * 2 + inner)
                for i, slot in enumerate(slots):
                    solved = (
                        middle[level, slot - 1] * inverse[level, slot - 1]
                        + factor[level, slot - 1] * carry[i]
                    )
                    carry[i] = solved
                    value = solved + source[level, slot - 1]
                    if last:
                        halves.append(value)
                    else:
                        state[level, slot] = value
            if last:
                below, above = halves
                base = pl.multiple_of(
                    (4 * LEV - 8) - (block * (4 * UNROLL) + pair * 8), 8
                )
                final[0, pl.ds(base, 8)] = jnp.where(low_row, above, pltpu.roll(below, 4, 0))
                final[1, pl.ds(base, 8)] = jnp.where(low_row, pltpu.roll(above, 4, 0), below)
        return carry

    def advance(step, carry):
        lax.fori_loop(0, LEV // UNROLL, functools.partial(descend, (1, 2, 3)), [zero] * 3)
        lax.fori_loop(0, LEV // UNROLL, functools.partial(ascend, (1, 2, 3), False), [zero] * 3)
        return carry

    lax.fori_loop(0, STEPS - 1, advance, 0)
    lax.fori_loop(0, LEV // UNROLL, functools.partial(descend, (2,)), [zero])
    final[0, pl.ds(4 * LEV, 24)] = jnp.zeros((24, LANES), F32)
    final[1, pl.ds(4 * LEV, 24)] = jnp.zeros((24, LANES), F32)
    lax.fori_loop(0, LEV // UNROLL, functools.partial(ascend, (2,), True), [zero])

    remote(final.at[1 - face], other, pair_sem.at[4], pair_sem.at[5], 1 - face, tile)
    moves[7].wait()
    moves[8].wait()
    choose = in_slot(cs_v[...]).T.astype(BF16)
    for source_of in range(2):
        if source_of == 0:
            values, tracer = final[face], face
        else:
            arrived(other, pair_sem.at[5])
            values, tracer = other[...], 1 - face
        high = values.astype(BF16)
        low = (values - high.astype(F32)).astype(BF16)
        pieces = column_dot(choose, high) + column_dot(choose, low)
        for part in range(3):
            stage_two[tracer, :, part, :] = pieces[:, part * LANES : (part + 1) * LANES]
    for part in range(6):
        send_two[:, part // 2, part % 2, :] = stage_two[part // 3, :, part % 3, :]

    def route_two(step, carry):
        to = lax.rem(tile + step, tiles)
        remote(send_two.at[to], land_two.at[tile], two_sem.at[0], two_sem.at[1], face, to)
        return carry

    lax.fori_loop(1, tiles, route_two, 0)
    self_two = pltpu.make_async_copy(send_two.at[tile], land_two.at[tile], local.at[13])
    self_two.start()
    place = in_slot(cp_v[...]).astype(BF16)
    self_two.wait()
    arrived(land_two.at[pl.ds(0, tiles - 1)], two_sem.at[1])
    for tracer in range(2):
        values = jnp.concatenate(
            [land_two[:, part // 2, part % 2, :] for part in range(3 * tracer, 3 * tracer + 3)],
            axis=1,
        )
        high = values.astype(BF16)
        low = (values - high.astype(F32)).astype(BF16)
        result = row_dot(high, place) + row_dot(low, place)
        out[tracer] = result[: 4 * LEV].reshape(LEV, 4, LANES)

    arrived(metas.at[pl.ds(0, 9)], meta_sem.at[0])
    arrived(own_adj.at[0], pair_sem.at[0])
    arrived(own_mis.at[0], pair_sem.at[2])
    arrived(land_one.at[0, pl.ds(0, tiles - 1)], one_sem.at[0])
    arrived(halo_adj, halo_sem.at[0])
    arrived(halo_edge, halo_sem.at[2])
    arrived(halo_mis, halo_sem.at[4])
    arrived(land_one.at[1], pass_sem.at[0])
    arrived(other, pair_sem.at[4])
    arrived(land_two.at[pl.ds(0, tiles - 1)], two_sem.at[0])


def per_device(
    fwd_tracers, fwd_kappa, send_order, recv_place, depth_levels, horiz_rate, adj_init, misfit,
    ctrl_send, ctrl_place,
):
    tiles = lax.axis_size("tile")
    anywhere = pl.BlockSpec(memory_space=pltpu.HBM)
    vmem = pltpu.VMEM
    dma = pltpu.SemaphoreType.DMA
    block = (LEV, 4, LANES)
    level_rows = (LEV, 3, 8, LANES)
    scratch = [
        pltpu.SMEM((LEV,), F32),
        vmem((2, LEV + 1, 4, LANES), BF16), vmem((LEV + 1, 4, LANES), BF16),
        vmem((1, LANES), I32), vmem((1, LANES), I32), vmem((4, LANES), I32),
        vmem((2,) + block, F32), vmem((2,) + block, F32),
        vmem((1, LANES), I32), vmem((1, LANES), I32),
        vmem((384, LANES), F32), vmem((tiles, 4, LANES), F32),
        vmem((tiles + 2, 4, LANES), BF16), vmem((2, tiles, 3, 4, LANES), BF16),
        vmem((2, 8, LANES), I32), vmem((10, 2, 8, LANES), I32),
        vmem((2,) + block, BF16), vmem((2,) + block, BF16), vmem((2, 2, LEV, 1, LANES), F32),
        vmem((4,) + block, BF16), vmem((4,) + block, BF16), vmem((4, LEV, 1, LANES), F32),
        vmem((2,) + block, F32), vmem((2,) + block, F32),
        vmem((2, 3, 384, LANES), F32), vmem((LEV, 5, 8, LANES), F32),
        vmem(level_rows, F32), vmem(level_rows, F32), vmem(level_rows, F32),
        vmem(level_rows, F32), vmem(level_rows, F32),
        vmem((2, 384, LANES), F32), vmem((384, LANES), F32),
        vmem((tiles, 3, 2, LANES), F32), vmem((tiles, 3, 2, LANES), F32),
        vmem((2, tiles, 3, LANES), F32),
        dma((14,)), dma((2,)), dma((2,)), dma((2,)), dma((6,)), dma((6,)), dma((2,)),
    ]
    return pl.pallas_call(
        functools.partial(kernel, tiles),
        out_shape=jax.ShapeDtypeStruct((2,) + block, F32),
        in_specs=[anywhere] * 10,
        out_specs=pl.BlockSpec(memory_space=pltpu.VMEM),
        scratch_shapes=scratch,
        compiler_params=pltpu.CompilerParams(
            collective_id=0, has_side_effects=True, vmem_limit_bytes=60 * 2**20
        ),
        cost_estimate=pl.CostEstimate(
            flops=10**9, bytes_accessed=4 * 2**20, transcendentals=10**5
        ),
    )(
        fwd_tracers, fwd_kappa, send_order, recv_place, depth_levels, horiz_rate, adj_init, misfit,
        ctrl_send, ctrl_place,
    )


def solution(mesh):
    placed = (
        P(None, None, None, ("face", "tile")),
        P(None, None, ("face", "tile")),
        P("face", "tile", None),
        P("face", "tile", None),
        P("tile", "face"),
        P(),
        P(None, None, "tile", "face"),
        P(None, None, "tile", "face"),
        P("face", "tile", None),
        P("face", "tile", None),
    )
    return jax.shard_map(
        per_device,
        mesh=mesh,
        in_specs=placed,
        out_specs=P(None, None, None, ("face", "tile")),
        check_vma=False,
    )
```

```python
import functools

import jax
import jax.numpy as jnp
from jax import lax
from jax.experimental import pallas as pl
from jax.experimental.pallas import tpu as pltpu
from jax.sharding import PartitionSpec as P

MESH = pl.DeviceIdType.MESH
F32 = jnp.float32
BF16 = jnp.bfloat16
I32 = jnp.int32
I16 = jnp.int16

LEV = 90
STEPS = 5
LANES = 128
UNROLL = 10
SWEEP = 90
CODE = 32000.0
SIDES = ((0, 1), (1, -1))


def ordered(slot, face0, face1):
    return (face0, face1) if slot % 2 == 0 else (face1, face0)


def stack_faces(slot, face0, face1):
    first, second = ordered(slot, face0, face1)
    return jnp.concatenate([first, second], axis=0)


def in_slot(index_array):
    rows = lax.broadcasted_iota(I32, (LANES, LANES), 0)
    return (rows == index_array).astype(F32)


def column_dot(lhs, rhs):
    return lax.dot_general(lhs, rhs, (((1,), (1,)), ((), ())), preferred_element_type=F32)


def row_dot(lhs, rhs):
    return lax.dot_general(lhs, rhs, (((0,), (1,)), ((), ())), preferred_element_type=F32)


def kernel(
    tiles,
    fwd, kap, send_order, recv_place, depth, rate_in, adj, mis, ctrl_send, ctrl_place,
    out,
    rate, fwd_v, kap_v, so_v, rp_v, depth_v, adj_v, mis_v, cs_v, cp_v,
    coup_v, stage, send_one, land_one,
    meta, metas, half_adj, half_mis, edge_adj, halo_adj, halo_mis, halo_edge, own_adj, own_mis,
    placed, state, middle, keep, factor, inverse, source,
    final, other, send_two, land_two, stage_pair, stage_two,
    local, meta_sem, one_sem, pass_sem, halo_sem, pair_sem, two_sem,
):
    tile = lax.axis_index("tile")
    face = lax.axis_index("face")
    barrier = pltpu.get_barrier_semaphore()

    def to_tile(shift):
        return lax.rem(tile + (shift + tiles), tiles)

    def greet(step, carry):
        pl.semaphore_signal(
            barrier, inc=1, device_id=(face, lax.rem(tile + step, tiles)), device_id_type=MESH
        )
        return carry

    for shift in (-2, -1, 0, 1, 2):
        pl.semaphore_signal(
            barrier, inc=1, device_id=(1 - face, to_tile(shift)), device_id_type=MESH
        )
    lax.fori_loop(1, tiles, greet, 0)

    moves = [
        pltpu.make_async_copy(src, dst, local.at[i])
        for i, (src, dst) in enumerate((
            (fwd, fwd_v.at[:, pl.ds(0, LEV)]),
            (kap, kap_v.at[pl.ds(0, LEV)]),
            (send_order.at[0], so_v),
            (recv_place.at[0], rp_v),
            (depth, depth_v),
            (adj, adj_v),
            (mis, mis_v),
            (ctrl_send.at[0], cs_v),
            (ctrl_place.at[0], cp_v),
            (adj.at[face], own_adj.at[face]),
            (mis.at[face], own_mis.at[face]),
            (rate_in, rate),
        ))
    ]
    for move in moves:
        move.start()
    fwd_v[0, LEV] = jnp.zeros((4, LANES), BF16)
    fwd_v[1, LEV] = jnp.zeros((4, LANES), BF16)
    kap_v[LEV] = jnp.zeros((4, LANES), BF16)
    coup_v[pl.ds(4 * LEV, 24)] = jnp.zeros((24, LANES), F32)
    stage[:, 3, :] = jnp.zeros((LANES, LANES), F32)

    for move in moves[:4]:
        move.wait()

    def density(level):
        return 0.8 * fwd_v[1, level].astype(F32) - 0.2 * fwd_v[0, level].astype(F32)

    def couple(block, carry):
        above, kappa_above = carry
        for pair in range(5):
            rows = []
            for half in range(2):
                level = block * 10 + pair * 2 + half + 1
                below = density(level)
                kappa_below = kap_v[level].astype(F32)
                contrast = below - above
                rows.append(
                    0.5 * (kappa_above + kappa_below) * (1.0 + 3.0 * jax.nn.sigmoid(-4.0 * contrast))
                )
                above, kappa_above = below, kappa_below
            coup_v[pl.ds(pl.multiple_of(block * 40 + pair * 8, 8), 8)] = jnp.concatenate(rows, axis=0)
        return above, kappa_above

    lax.fori_loop(0, LEV // 10, couple, (density(0), kap_v[0].astype(F32)))

    pick = in_slot(so_v[...]).T.astype(BF16)
    pieces = column_dot(pick, coup_v[...].astype(BF16))
    for part in range(3):
        stage[:, part, :] = pieces[:, part * LANES : (part + 1) * LANES]
    packed = stage[...].astype(BF16)
    send_one[pl.ds(1, tiles)] = packed
    send_one[0] = packed[tiles - 1]
    send_one[tiles + 1] = packed[0]

    moves[4].wait()
    meta[0] = jnp.concatenate([depth_v[...], depth_v[...]], axis=0)
    meta[1] = jnp.broadcast_to(rp_v[...], (8, LANES))
    metas[4 + face] = meta[...]
    moves[5].wait()
    for tracer in range(2):
        half_adj[tracer] = adj_v[tracer].astype(BF16)
        edge_adj[0, tracer] = adj_v[tracer, :, 3:4, :]
        edge_adj[1, tracer] = adj_v[tracer, :, 0:1, :]
    moves[6].wait()
    for tracer in range(2):
        half_mis[tracer] = mis_v[tracer].astype(BF16)

    pl.semaphore_wait(barrier, tiles + 4)

    def remote(src, dst, send_sem, recv_sem, to_face, to):
        pltpu.make_async_remote_copy(
            src_ref=src, dst_ref=dst, send_sem=send_sem, recv_sem=recv_sem,
            device_id=(to_face, to), device_id_type=MESH,
        ).start()

    for shift in (-1, 1, -2, 2):
        for tracer in range(2):
            remote(
                meta, metas.at[2 * (2 - shift) + face],
                meta_sem.at[0], meta_sem.at[1], tracer, to_tile(shift),
            )
    remote(meta, metas.at[4 + face], meta_sem.at[0], meta_sem.at[1], 1 - face, tile)
    remote(
        adj.at[1 - face], own_adj.at[face], pair_sem.at[0], pair_sem.at[1], 1 - face, tile
    )
    remote(
        mis.at[1 - face], own_mis.at[face], pair_sem.at[2], pair_sem.at[3], 1 - face, tile
    )

    def route_one(step, carry):
        to = lax.rem(tile + step, tiles)
        remote(
            send_one.at[pl.ds(to, 3)], land_one.at[0, tile], one_sem.at[0], one_sem.at[1], face, to
        )
        return carry

    lax.fori_loop(1, tiles, route_one, 0)
    self_one = pltpu.make_async_copy(
        send_one.at[pl.ds(tile, 3)], land_one.at[0, tile], local.at[12]
    )
    self_one.start()
    for side, shift in SIDES:
        for tracer in range(2):
            remote(
                half_adj.at[tracer], halo_adj.at[2 * side + face],
                halo_sem.at[0], halo_sem.at[1], tracer, to_tile(shift),
            )
            remote(
                edge_adj.at[side, tracer], halo_edge.at[2 * side + face],
                halo_sem.at[2], halo_sem.at[3], tracer, to_tile(2 * shift),
            )
    for side, shift in SIDES:
        for tracer in range(2):
            remote(
                half_mis.at[tracer], halo_mis.at[2 * side + face],
                halo_sem.at[4], halo_sem.at[5], tracer, to_tile(shift),
            )

    def arrived(ref, semaphore):
        pltpu.make_async_copy(ref, ref, semaphore).wait()

    row = lax.broadcasted_iota(I32, (8, LANES), 0)
    lane = lax.broadcasted_iota(I32, (8, LANES), 1)
    cell = row % 4
    first_cell, last_cell = cell == 0, cell == 3
    first_lane, last_lane = lane == 0, lane == LANES - 1
    low_lane, low_row = lane < LANES // 2, row < 4
    seam_even = low_lane == low_row
    seam_odd = low_lane != low_row

    def neighbours(slot, west, here, east):
        seam = jnp.where(seam_even if slot % 2 == 0 else seam_odd, pltpu.roll(here, 4, 0), 0.0)
        return (
            pltpu.roll(jnp.where(first_cell, east, here), 7, 0),
            pltpu.roll(jnp.where(last_cell, west, here), 1, 0),
            pltpu.roll(jnp.where(first_lane, seam, here), LANES - 1, 1),
            pltpu.roll(jnp.where(last_lane, seam, here), 1, 1),
        )

    arrived(metas.at[pl.ds(0, 9)], meta_sem.at[1])
    depths = []
    for slot in range(5):
        at = tile + (slot - 2)
        inside = jnp.logical_and(at >= 0, at < tiles).astype(F32)
        first, second = ordered(slot, metas[2 * slot, 0], metas[2 * slot + 1, 0])
        depths.append(jnp.where(low_row, first, second).astype(F32) * inside)
    around = [
        neighbours(slot, depths[slot - 1], depths[slot], depths[slot + 1]) for slot in (1, 2, 3)
    ]

    def wet(level, slot):
        return level.astype(F32) < depths[slot]

    def prepare(block, carry):
        for inner in range(5):
            level = block * 5 + inner
            at = level.astype(F32)
            speed = rate[level]
            for slot in (1, 2, 3):
                count = jnp.zeros((8, LANES), F32)
                for beside in around[slot - 1]:
                    count = count + jnp.where(at < beside, 1.0, 0.0)
                keep[level, slot - 1] = 1.0 - speed * count
        return carry

    moves[11].wait()
    lax.fori_loop(0, LEV // 5, prepare, 0)

    self_one.wait()
    arrived(land_one.at[0, pl.ds(0, tiles - 1)], one_sem.at[1])
    remote(land_one.at[0], land_one.at[1], pass_sem.at[0], pass_sem.at[1], 1 - face, tile)
    for source_of in range(2):
        if source_of == 1:
            moves[9].wait()
            arrived(own_adj.at[0], pair_sem.at[1])
            arrived(halo_adj, halo_sem.at[1])
            arrived(halo_edge, halo_sem.at[3])

            def begin(block, carry):
                for inner in range(5):
                    level = block * 5 + inner
                    tile_of = {
                        1: stack_faces(1, halo_adj[0, level].astype(F32), halo_adj[1, level].astype(F32)),
                        2: stack_faces(2, own_adj[0, level], own_adj[1, level]),
                        3: stack_faces(3, halo_adj[2, level].astype(F32), halo_adj[3, level].astype(F32)),
                        0: jnp.where(low_row, halo_edge[0, level], halo_edge[1, level]),
                        4: jnp.where(low_row, halo_edge[2, level], halo_edge[3, level]),
                    }
                    for slot in range(5):
                        state[level, slot] = jnp.where(wet(level, slot), tile_of[slot], 0.0)
                return carry

            lax.fori_loop(0, LEV // 5, begin, 0)
            arrived(land_one.at[1], pass_sem.at[1])
        which = face if source_of == 0 else 1 - face
        for part in range(3):
            stage[...] = land_one[source_of, :, part].astype(F32)
            held = jnp.concatenate([stage[:, i, :] for i in range(3)], axis=1).astype(BF16)
            place = in_slot(metas[2 * (part + 1) + which, 1][0:1, :]).astype(BF16)
            placed[which, part] = row_dot(held, place)

    one = jnp.ones((8, LANES), F32)

    def eliminate(block, carry):
        carry = [(upper / lower, one) for upper, lower in carry]
        for pair in range(UNROLL // 2):
            base = pl.multiple_of(block * (4 * UNROLL) + pair * 8, 8)
            for slot in (1, 2, 3):
                first, second = ordered(
                    slot, placed[0, slot - 1, pl.ds(base, 8)], placed[1, slot - 1, pl.ds(base, 8)]
                )
                couplings = (
                    jnp.where(low_row, first, pltpu.roll(second, 4, 0)),
                    jnp.where(low_row, pltpu.roll(first, 4, 0), second),
                )
                upper, lower = carry[slot - 1]
                for half in range(2):
                    level = block * UNROLL + pair * 2 + half
                    weight = jnp.where(
                        (level + 1).astype(F32) < depths[slot], couplings[half], 0.0
                    )
                    next_lower = upper + weight * lower
                    next_upper = next_lower + weight * upper
                    ratio = lower / next_lower
                    factor[level, slot - 1] = weight * ratio
                    inverse[level, slot - 1] = jnp.where(wet(level, slot), ratio, 0.0)
                    upper, lower = next_upper, next_lower
                carry[slot - 1] = (upper, lower)
        return carry

    lax.fori_loop(0, LEV // UNROLL, eliminate, [(one, one)] * 3)

    zero = jnp.zeros((8, LANES), F32)

    def descend(slots, block, carry):
        carry = list(carry)
        for inner in range(SWEEP):
            level = block * SWEEP + inner
            speed = rate[level]
            tile_of = {
                slot: state[level, slot] for slot in range(slots[0] - 1, slots[-1] + 2)
            }
            for i, slot in enumerate(slots):
                east, west, north, south = neighbours(
                    slot, tile_of[slot - 1], tile_of[slot], tile_of[slot + 1]
                )
                spread = keep[level, slot - 1] * tile_of[slot] + speed * (
                    (east + west) + (north + south)
                )
                value = spread + carry[i]
                middle[level, slot - 1] = value
                carry[i] = factor[level, slot - 1] * value
        return carry

    def ascend(slots, last, block, carry):
        carry = list(carry)
        for pair in range(SWEEP // 2):
            halves = []
            for inner in range(2):
                level = (LEV - 1) - (block * SWEEP + pair * 2 + inner)
                for i, slot in enumerate(slots):
                    solved = (
                        middle[level, slot - 1] * inverse[level, slot - 1]
                        + factor[level, slot - 1] * carry[i]
                    )
                    carry[i] = solved
                    value = solved + source[level, slot - 1]
                    if last:
                        halves.append(value)
                    else:
                        state[level, slot] = value
            if last:
                below, above = halves
                base = pl.multiple_of(
                    (4 * LEV - 8) - (block * (4 * SWEEP) + pair * 8), 8
                )
                final[0, pl.ds(base, 8)] = jnp.where(low_row, above, pltpu.roll(below, 4, 0))
                final[1, pl.ds(base, 8)] = jnp.where(low_row, pltpu.roll(above, 4, 0), below)
        return carry

    def advance(step, carry):
        lax.fori_loop(0, LEV // SWEEP, functools.partial(descend, (1, 2, 3)), [zero] * 3)
        lax.fori_loop(0, LEV // SWEEP, functools.partial(ascend, (1, 2, 3), False), [zero] * 3)
        return carry

    sweep_down = functools.partial(descend, (1, 2, 3))
    lax.fori_loop(0, LEV // SWEEP, sweep_down, [zero] * 3)
    moves[10].wait()
    arrived(own_mis.at[0], pair_sem.at[3])
    arrived(halo_mis, halo_sem.at[5])

    def drive(block, carry):
        for inner in range(5):
            level = block * 5 + inner
            tile_of = {
                1: stack_faces(1, halo_mis[0, level].astype(F32), halo_mis[1, level].astype(F32)),
                2: stack_faces(2, own_mis[0, level], own_mis[1, level]),
                3: stack_faces(3, halo_mis[2, level].astype(F32), halo_mis[3, level].astype(F32)),
            }
            for slot in (1, 2, 3):
                source[level, slot - 1] = jnp.where(wet(level, slot), tile_of[slot], 0.0)
        return carry

    lax.fori_loop(0, LEV // 5, drive, 0)

    lax.fori_loop(0, LEV // SWEEP, functools.partial(ascend, (1, 2, 3), False), [zero] * 3)
    lax.fori_loop(1, STEPS - 1, advance, 0)
    lax.fori_loop(0, LEV // SWEEP, functools.partial(descend, (2,)), [zero])
    final[0, pl.ds(4 * LEV, 24)] = jnp.zeros((24, LANES), F32)
    final[1, pl.ds(4 * LEV, 24)] = jnp.zeros((24, LANES), F32)
    lax.fori_loop(0, LEV // SWEEP, functools.partial(ascend, (2,), True), [zero])

    remote(final.at[1 - face], other, pair_sem.at[4], pair_sem.at[5], 1 - face, tile)
    moves[7].wait()
    moves[8].wait()
    choose = in_slot(cs_v[...]).T.astype(BF16)
    end_lane = lax.broadcasted_iota(I32, (LANES, LANES), 1) == LANES - 1
    for source_of in range(2):
        if source_of == 0:
            values, tracer = final[face], face
        else:
            arrived(other, pair_sem.at[5])
            values, tracer = other[...], 1 - face
        high = values.astype(BF16)
        low = (values - high.astype(F32)).astype(BF16)
        pieces = column_dot(choose, high) + column_dot(choose, low)
        largest = jnp.max(jnp.abs(pieces), axis=1, keepdims=True)
        octave = jnp.ceil(4.0 * jnp.log2(jnp.maximum(largest, 1e-33)) + 0.01)
        codes = jnp.floor(pieces * (CODE / jnp.exp2(0.25 * octave)) + 0.5)
        for part in range(3):
            column = codes[:, part * LANES : (part + 1) * LANES]
            if part == 2:
                column = jnp.where(end_lane, octave, column)
            stage_two[tracer, :, part, :] = column
    for part in range(6):
        stage_pair[:, part // 2, part % 2, :] = stage_two[part // 3, :, part % 3, :]
    send_two[...] = stage_pair[...].astype(I32).astype(I16)

    def route_two(step, carry):
        to = lax.rem(tile + step, tiles)
        remote(send_two.at[to], land_two.at[tile], two_sem.at[0], two_sem.at[1], face, to)
        return carry

    lax.fori_loop(1, tiles, route_two, 0)
    self_two = pltpu.make_async_copy(send_two.at[tile], land_two.at[tile], local.at[13])
    self_two.start()
    place = in_slot(cp_v[...]).astype(BF16)
    self_two.wait()
    arrived(land_two.at[pl.ds(0, tiles - 1)], two_sem.at[1])
    stage_pair[...] = land_two[...].astype(I32).astype(F32)
    for tracer in range(2):
        values = jnp.concatenate(
            [stage_pair[:, part // 2, part % 2, :] for part in range(3 * tracer, 3 * tracer + 3)],
            axis=1,
        )
        octave = values[:, 3 * LANES - 1 :]
        values = values * (jnp.exp2(0.25 * octave) * (1.0 / CODE))
        high = values.astype(BF16)
        low = (values - high.astype(F32)).astype(BF16)
        result = row_dot(high, place) + row_dot(low, place)
        out[tracer] = result[: 4 * LEV].reshape(LEV, 4, LANES)

    arrived(metas.at[pl.ds(0, 9)], meta_sem.at[0])
    arrived(own_adj.at[0], pair_sem.at[0])
    arrived(own_mis.at[0], pair_sem.at[2])
    arrived(land_one.at[0, pl.ds(0, tiles - 1)], one_sem.at[0])
    arrived(halo_adj, halo_sem.at[0])
    arrived(halo_edge, halo_sem.at[2])
    arrived(halo_mis, halo_sem.at[4])
    arrived(land_one.at[1], pass_sem.at[0])
    arrived(other, pair_sem.at[4])
    arrived(land_two.at[pl.ds(0, tiles - 1)], two_sem.at[0])


def per_device(
    fwd_tracers, fwd_kappa, send_order, recv_place, depth_levels, horiz_rate, adj_init, misfit,
    ctrl_send, ctrl_place,
):
    tiles = lax.axis_size("tile")
    anywhere = pl.BlockSpec(memory_space=pltpu.HBM)
    vmem = pltpu.VMEM
    dma = pltpu.SemaphoreType.DMA
    block = (LEV, 4, LANES)
    level_rows = (LEV, 3, 8, LANES)
    scratch = [
        pltpu.SMEM((LEV,), F32),
        vmem((2, LEV + 1, 4, LANES), BF16), vmem((LEV + 1, 4, LANES), BF16),
        vmem((1, LANES), I32), vmem((1, LANES), I32), vmem((4, LANES), I32),
        vmem((2,) + block, F32), vmem((2,) + block, F32),
        vmem((1, LANES), I32), vmem((1, LANES), I32),
        vmem((384, LANES), F32), vmem((tiles, 4, LANES), F32),
        vmem((tiles + 2, 4, LANES), BF16), vmem((2, tiles, 3, 4, LANES), BF16),
        vmem((2, 8, LANES), I32), vmem((10, 2, 8, LANES), I32),
        vmem((2,) + block, BF16), vmem((2,) + block, BF16), vmem((2, 2, LEV, 1, LANES), F32),
        vmem((4,) + block, BF16), vmem((4,) + block, BF16), vmem((4, LEV, 1, LANES), F32),
        vmem((2,) + block, F32), vmem((2,) + block, F32),
        vmem((2, 3, 384, LANES), F32), vmem((LEV, 5, 8, LANES), F32),
        vmem(level_rows, F32), vmem(level_rows, F32), vmem(level_rows, F32),
        vmem(level_rows, F32), vmem(level_rows, F32),
        vmem((2, 384, LANES), F32), vmem((384, LANES), F32),
        vmem((tiles, 3, 2, LANES), I16), vmem((tiles, 3, 2, LANES), I16),
        vmem((tiles, 3, 2, LANES), F32),
        vmem((2, tiles, 3, LANES), F32),
        dma((14,)), dma((2,)), dma((2,)), dma((2,)), dma((6,)), dma((6,)), dma((2,)),
    ]
    return pl.pallas_call(
        functools.partial(kernel, tiles),
        out_shape=jax.ShapeDtypeStruct((2,) + block, F32),
        in_specs=[anywhere] * 10,
        out_specs=pl.BlockSpec(memory_space=pltpu.VMEM),
        scratch_shapes=scratch,
        compiler_params=pltpu.CompilerParams(
            collective_id=0, has_side_effects=True, vmem_limit_bytes=60 * 2**20
        ),
        cost_estimate=pl.CostEstimate(
            flops=10**9, bytes_accessed=4 * 2**20, transcendentals=10**5
        ),
    )(
        fwd_tracers, fwd_kappa, send_order, recv_place, depth_levels, horiz_rate, adj_init, misfit,
        ctrl_send, ctrl_place,
    )


def solution(mesh):
    placed = (
        P(None, None, None, ("face", "tile")),
        P(None, None, ("face", "tile")),
        P("face", "tile", None),
        P("face", "tile", None),
        P("tile", "face"),
        P(),
        P(None, None, "tile", "face"),
        P(None, None, "tile", "face"),
        P("face", "tile", None),
        P("face", "tile", None),
    )
    return jax.shard_map(
        per_device,
        mesh=mesh,
        in_specs=placed,
        out_specs=P(None, None, None, ("face", "tile")),
        check_vma=False,
    )
```

```python
import functools

import jax
import jax.numpy as jnp
from jax import lax
from jax.experimental import pallas as pl
from jax.experimental.pallas import tpu as pltpu
from jax.sharding import PartitionSpec as P

MESH = pl.DeviceIdType.MESH
F32 = jnp.float32
BF16 = jnp.bfloat16
I32 = jnp.int32
I16 = jnp.int16

LEV = 90
STEPS = 5
LANES = 128
UNROLL = 10
SWEEP = 90
CODE = 32000.0
SIDES = ((0, 1), (1, -1))


def ordered(slot, face0, face1):
    return (face0, face1) if slot % 2 == 0 else (face1, face0)


def stack_faces(slot, face0, face1):
    first, second = ordered(slot, face0, face1)
    return jnp.concatenate([first, second], axis=0)


def in_slot(index_array):
    rows = lax.broadcasted_iota(I32, (LANES, LANES), 0)
    return (rows == index_array).astype(F32)


def column_dot(lhs, rhs):
    return lax.dot_general(lhs, rhs, (((1,), (1,)), ((), ())), preferred_element_type=F32)


def row_dot(lhs, rhs):
    return lax.dot_general(lhs, rhs, (((0,), (1,)), ((), ())), preferred_element_type=F32)


def kernel(
    tiles,
    fwd, kap, send_order, recv_place, depth, rate_in, adj, mis, ctrl_send, ctrl_place,
    out,
    rate, fwd_v, kap_v, so_v, rp_v, depth_v, adj_v, mis_v, cs_v, cp_v,
    coup_v, stage, send_one, land_one,
    meta, metas, half_adj, half_mis, edge_adj, halo_adj, halo_mis, halo_edge, own_adj, own_mis,
    placed, state, middle, keep, factor, inverse, source,
    final, other, send_two, land_two, stage_pair,
    local, meta_sem, one_sem, pass_sem, halo_sem, pair_sem, two_sem,
):
    tile = lax.axis_index("tile")
    face = lax.axis_index("face")
    barrier = pltpu.get_barrier_semaphore()

    def to_tile(shift):
        return lax.rem(tile + (shift + tiles), tiles)

    def greet(step, carry):
        pl.semaphore_signal(
            barrier, inc=1, device_id=(face, lax.rem(tile + step, tiles)), device_id_type=MESH
        )
        return carry

    for shift in (-2, -1, 0, 1, 2):
        pl.semaphore_signal(
            barrier, inc=1, device_id=(1 - face, to_tile(shift)), device_id_type=MESH
        )
    lax.fori_loop(1, tiles, greet, 0)

    moves = [
        pltpu.make_async_copy(src, dst, local.at[i])
        for i, (src, dst) in enumerate((
            (fwd, fwd_v.at[:, pl.ds(0, LEV)]),
            (kap, kap_v.at[pl.ds(0, LEV)]),
            (send_order.at[0], so_v),
            (recv_place.at[0], rp_v),
            (depth, depth_v),
            (adj, adj_v),
            (mis, mis_v),
            (ctrl_send.at[0], cs_v),
            (ctrl_place.at[0], cp_v),
            (adj.at[face], own_adj.at[face]),
            (mis.at[face], own_mis.at[face]),
            (rate_in, rate),
        ))
    ]
    for move in moves:
        move.start()
    fwd_v[0, LEV] = jnp.zeros((4, LANES), BF16)
    fwd_v[1, LEV] = jnp.zeros((4, LANES), BF16)
    kap_v[LEV] = jnp.zeros((4, LANES), BF16)
    coup_v[pl.ds(4 * LEV, 24)] = jnp.zeros((24, LANES), F32)
    stage[:, 4, 1, :] = jnp.zeros((LANES, LANES), F32)

    for move in moves[:4]:
        move.wait()

    def density(level):
        return 0.8 * fwd_v[1, level].astype(F32) - 0.2 * fwd_v[0, level].astype(F32)

    def couple(block, carry):
        above, kappa_above = carry
        for pair in range(5):
            rows = []
            for half in range(2):
                level = block * 10 + pair * 2 + half + 1
                below = density(level)
                kappa_below = kap_v[level].astype(F32)
                contrast = below - above
                rows.append(
                    0.5 * (kappa_above + kappa_below) * (1.0 + 3.0 * jax.nn.sigmoid(-4.0 * contrast))
                )
                above, kappa_above = below, kappa_below
            coup_v[pl.ds(pl.multiple_of(block * 40 + pair * 8, 8), 8)] = jnp.concatenate(rows, axis=0)
        return above, kappa_above

    lax.fori_loop(0, LEV // 10, couple, (density(0), kap_v[0].astype(F32)))

    pick = in_slot(so_v[...]).T.astype(BF16)
    pieces = column_dot(pick, coup_v[...].astype(BF16))
    for beside in range(3):
        moved = pieces if beside == 1 else pltpu.roll(pieces, (1 - beside) % tiles, 0)
        for part in range(3):
            at = 3 * beside + part
            stage[:, at // 2, at % 2, :] = moved[:, part * LANES : (part + 1) * LANES]
    send_one[...] = stage[...].astype(BF16)

    moves[4].wait()
    meta[0] = jnp.concatenate([depth_v[...], depth_v[...]], axis=0)
    meta[1] = jnp.broadcast_to(rp_v[...], (8, LANES))
    metas[4 + face] = meta[...]
    moves[5].wait()
    for tracer in range(2):
        half_adj[tracer] = adj_v[tracer].astype(BF16)

    def outline(block, carry):
        for pair in range(3):
            level = 2 * (block * 3 + pair)
            for tracer in range(2):
                for side, line in ((0, 3), (1, 0)):
                    rows = [adj_v[tracer, level + half, line : line + 1, :] for half in range(2)]
                    edge_adj[side, tracer, block * 3 + pair] = jnp.concatenate(
                        rows, axis=0
                    ).astype(BF16)
        return carry

    lax.fori_loop(0, LEV // 6, outline, 0)
    moves[6].wait()
    for tracer in range(2):
        half_mis[tracer] = mis_v[tracer].astype(BF16)

    pl.semaphore_wait(barrier, tiles + 4)

    def remote(src, dst, send_sem, recv_sem, to_face, to):
        pltpu.make_async_remote_copy(
            src_ref=src, dst_ref=dst, send_sem=send_sem, recv_sem=recv_sem,
            device_id=(to_face, to), device_id_type=MESH,
        ).start()

    for shift in (-1, 1, -2, 2):
        for tracer in range(2):
            remote(
                meta, metas.at[2 * (2 - shift) + face],
                meta_sem.at[0], meta_sem.at[1], tracer, to_tile(shift),
            )
    remote(meta, metas.at[4 + face], meta_sem.at[0], meta_sem.at[1], 1 - face, tile)
    remote(
        adj.at[1 - face], own_adj.at[face], pair_sem.at[0], pair_sem.at[1], 1 - face, tile
    )
    remote(
        mis.at[1 - face], own_mis.at[face], pair_sem.at[2], pair_sem.at[3], 1 - face, tile
    )

    def route_one(step, carry):
        to = lax.rem(tile + step, tiles)
        remote(
            send_one.at[to], land_one.at[0, tile], one_sem.at[0], one_sem.at[1], face, to
        )
        return carry

    lax.fori_loop(1, tiles, route_one, 0)
    self_one = pltpu.make_async_copy(
        send_one.at[tile], land_one.at[0, tile], local.at[12]
    )
    self_one.start()
    for side, shift in SIDES:
        for tracer in range(2):
            remote(
                half_adj.at[tracer], halo_adj.at[2 * side + face],
                halo_sem.at[0], halo_sem.at[1], tracer, to_tile(shift),
            )
            remote(
                edge_adj.at[side, tracer], halo_edge.at[2 * side + face],
                halo_sem.at[2], halo_sem.at[3], tracer, to_tile(2 * shift),
            )
    for side, shift in SIDES:
        for tracer in range(2):
            remote(
                half_mis.at[tracer], halo_mis.at[2 * side + face],
                halo_sem.at[4], halo_sem.at[5], tracer, to_tile(shift),
            )

    def arrived(ref, semaphore):
        pltpu.make_async_copy(ref, ref, semaphore).wait()

    row = lax.broadcasted_iota(I32, (8, LANES), 0)
    lane = lax.broadcasted_iota(I32, (8, LANES), 1)
    cell = row % 4
    first_cell, last_cell = cell == 0, cell == 3
    first_lane, last_lane = lane == 0, lane == LANES - 1
    low_lane, low_row = lane < LANES // 2, row < 4
    seam_even = low_lane == low_row
    seam_odd = low_lane != low_row

    def neighbours(slot, west, here, east):
        seam = jnp.where(seam_even if slot % 2 == 0 else seam_odd, pltpu.roll(here, 4, 0), 0.0)
        return (
            pltpu.roll(jnp.where(first_cell, east, here), 7, 0),
            pltpu.roll(jnp.where(last_cell, west, here), 1, 0),
            pltpu.roll(jnp.where(first_lane, seam, here), LANES - 1, 1),
            pltpu.roll(jnp.where(last_lane, seam, here), 1, 1),
        )

    arrived(metas.at[pl.ds(0, 9)], meta_sem.at[1])
    depths = []
    for slot in range(5):
        at = tile + (slot - 2)
        inside = jnp.logical_and(at >= 0, at < tiles).astype(F32)
        first, second = ordered(slot, metas[2 * slot, 0], metas[2 * slot + 1, 0])
        depths.append(jnp.where(low_row, first, second).astype(F32) * inside)
    around = [
        neighbours(slot, depths[slot - 1], depths[slot], depths[slot + 1]) for slot in (1, 2, 3)
    ]

    def wet(level, slot):
        return level.astype(F32) < depths[slot]

    def prepare(block, carry):
        for inner in range(5):
            level = block * 5 + inner
            at = level.astype(F32)
            speed = rate[level]
            for slot in (1, 2, 3):
                count = jnp.zeros((8, LANES), F32)
                for beside in around[slot - 1]:
                    count = count + jnp.where(at < beside, 1.0, 0.0)
                keep[level, slot - 1] = 1.0 - speed * count
        return carry

    moves[11].wait()
    lax.fori_loop(0, LEV // 5, prepare, 0)

    self_one.wait()
    arrived(land_one.at[0, pl.ds(0, tiles - 1)], one_sem.at[1])
    remote(land_one.at[0], land_one.at[1], pass_sem.at[0], pass_sem.at[1], 1 - face, tile)
    for source_of in range(2):
        if source_of == 1:
            moves[9].wait()
            arrived(own_adj.at[0], pair_sem.at[1])
            arrived(halo_adj, halo_sem.at[1])
            arrived(halo_edge, halo_sem.at[3])

            def begin(block, carry):
                for inner in range(6):
                    level = block * 6 + inner
                    lines = [
                        halo_edge[i, block * 3 + inner // 2].astype(F32)[inner % 2 : inner % 2 + 1]
                        for i in range(4)
                    ]
                    tile_of = {
                        1: stack_faces(1, halo_adj[0, level].astype(F32), halo_adj[1, level].astype(F32)),
                        2: stack_faces(2, own_adj[0, level], own_adj[1, level]),
                        3: stack_faces(3, halo_adj[2, level].astype(F32), halo_adj[3, level].astype(F32)),
                        0: jnp.where(low_row, lines[0], lines[1]),
                        4: jnp.where(low_row, lines[2], lines[3]),
                    }
                    for slot in range(5):
                        state[level, slot] = jnp.where(wet(level, slot), tile_of[slot], 0.0)
                return carry

            lax.fori_loop(0, LEV // 6, begin, 0)
            arrived(land_one.at[1], pass_sem.at[1])
        which = face if source_of == 0 else 1 - face
        stage[...] = land_one[source_of].astype(F32)
        for part in range(3):
            held = jnp.concatenate(
                [stage[:, at // 2, at % 2, :] for at in range(3 * part, 3 * part + 3)], axis=1
            ).astype(BF16)
            place = in_slot(metas[2 * (part + 1) + which, 1][0:1, :]).astype(BF16)
            placed[which, part] = row_dot(held, place)

    one = jnp.ones((8, LANES), F32)

    def eliminate(block, carry):
        carry = [(upper / lower, one) for upper, lower in carry]
        for pair in range(UNROLL // 2):
            base = pl.multiple_of(block * (4 * UNROLL) + pair * 8, 8)
            for slot in (1, 2, 3):
                first, second = ordered(
                    slot, placed[0, slot - 1, pl.ds(base, 8)], placed[1, slot - 1, pl.ds(base, 8)]
                )
                couplings = (
                    jnp.where(low_row, first, pltpu.roll(second, 4, 0)),
                    jnp.where(low_row, pltpu.roll(first, 4, 0), second),
                )
                upper, lower = carry[slot - 1]
                for half in range(2):
                    level = block * UNROLL + pair * 2 + half
                    weight = jnp.where(
                        (level + 1).astype(F32) < depths[slot], couplings[half], 0.0
                    )
                    next_lower = upper + weight * lower
                    next_upper = next_lower + weight * upper
                    ratio = lower / next_lower
                    factor[level, slot - 1] = weight * ratio
                    inverse[level, slot - 1] = jnp.where(wet(level, slot), ratio, 0.0)
                    upper, lower = next_upper, next_lower
                carry[slot - 1] = (upper, lower)
        return carry

    lax.fori_loop(0, LEV // UNROLL, eliminate, [(one, one)] * 3)

    zero = jnp.zeros((8, LANES), F32)

    def descend(slots, block, carry):
        carry = list(carry)
        for inner in range(SWEEP):
            level = block * SWEEP + inner
            speed = rate[level]
            tile_of = {
                slot: state[level, slot] for slot in range(slots[0] - 1, slots[-1] + 2)
            }
            for i, slot in enumerate(slots):
                east, west, north, south = neighbours(
                    slot, tile_of[slot - 1], tile_of[slot], tile_of[slot + 1]
                )
                spread = keep[level, slot - 1] * tile_of[slot] + speed * (
                    (east + west) + (north + south)
                )
                value = spread + carry[i]
                middle[level, slot - 1] = value
                carry[i] = factor[level, slot - 1] * value
        return carry

    def ascend(slots, last, block, carry):
        carry = list(carry)
        for pair in range(SWEEP // 2):
            halves = []
            for inner in range(2):
                level = (LEV - 1) - (block * SWEEP + pair * 2 + inner)
                for i, slot in enumerate(slots):
                    solved = (
                        middle[level, slot - 1] * inverse[level, slot - 1]
                        + factor[level, slot - 1] * carry[i]
                    )
                    carry[i] = solved
                    value = solved + source[level, slot - 1]
                    if last:
                        halves.append(value)
                    else:
                        state[level, slot] = value
            if last:
                below, above = halves
                base = pl.multiple_of(
                    (4 * LEV - 8) - (block * (4 * SWEEP) + pair * 8), 8
                )
                final[0, pl.ds(base, 8)] = jnp.where(low_row, above, pltpu.roll(below, 4, 0))
                final[1, pl.ds(base, 8)] = jnp.where(low_row, pltpu.roll(above, 4, 0), below)
        return carry

    def advance(step, carry):
        lax.fori_loop(0, LEV // SWEEP, functools.partial(descend, (1, 2, 3)), [zero] * 3)
        lax.fori_loop(0, LEV // SWEEP, functools.partial(ascend, (1, 2, 3), False), [zero] * 3)
        return carry

    sweep_down = functools.partial(descend, (1, 2, 3))
    lax.fori_loop(0, LEV // SWEEP, sweep_down, [zero] * 3)
    moves[10].wait()
    arrived(own_mis.at[0], pair_sem.at[3])
    arrived(halo_mis, halo_sem.at[5])

    def drive(block, carry):
        for inner in range(5):
            level = block * 5 + inner
            tile_of = {
                1: stack_faces(1, halo_mis[0, level].astype(F32), halo_mis[1, level].astype(F32)),
                2: stack_faces(2, own_mis[0, level], own_mis[1, level]),
                3: stack_faces(3, halo_mis[2, level].astype(F32), halo_mis[3, level].astype(F32)),
            }
            for slot in (1, 2, 3):
                source[level, slot - 1] = jnp.where(wet(level, slot), tile_of[slot], 0.0)
        return carry

    lax.fori_loop(0, LEV // 5, drive, 0)

    lax.fori_loop(0, LEV // SWEEP, functools.partial(ascend, (1, 2, 3), False), [zero] * 3)
    lax.fori_loop(1, STEPS - 1, advance, 0)
    lax.fori_loop(0, LEV // SWEEP, functools.partial(descend, (2,)), [zero])
    final[0, pl.ds(4 * LEV, 24)] = jnp.zeros((24, LANES), F32)
    final[1, pl.ds(4 * LEV, 24)] = jnp.zeros((24, LANES), F32)
    lax.fori_loop(0, LEV // SWEEP, functools.partial(ascend, (2,), True), [zero])

    remote(final.at[1 - face], other, pair_sem.at[4], pair_sem.at[5], 1 - face, tile)
    moves[7].wait()
    moves[8].wait()
    choose = in_slot(cs_v[...]).T.astype(BF16)
    end_lane = lax.broadcasted_iota(I32, (LANES, LANES), 1) == LANES - 1
    for source_of in range(2):
        if source_of == 0:
            values = final[face]
        else:
            arrived(other, pair_sem.at[5])
            values = other[...]
        high = values.astype(BF16)
        low = (values - high.astype(F32)).astype(BF16)
        pieces = column_dot(choose, high) + column_dot(choose, low)
        largest = jnp.max(jnp.abs(pieces), axis=1, keepdims=True)
        octave = jnp.ceil(4.0 * jnp.log2(jnp.maximum(largest, 1e-33)) + 0.01)
        codes = jnp.floor(pieces * (CODE / jnp.exp2(0.25 * octave)) + 0.5)
        for part in range(3):
            column = codes[:, part * LANES : (part + 1) * LANES]
            if part == 2:
                column = jnp.where(end_lane, octave, column)
            stage_pair[:, (3 * source_of + part) // 2, (3 * source_of + part) % 2, :] = column
    send_two[...] = stage_pair[...].astype(I32).astype(I16)

    def route_two(step, carry):
        to = lax.rem(tile + step, tiles)
        remote(send_two.at[to], land_two.at[tile], two_sem.at[0], two_sem.at[1], face, to)
        return carry

    lax.fori_loop(1, tiles, route_two, 0)
    self_two = pltpu.make_async_copy(send_two.at[tile], land_two.at[tile], local.at[13])
    self_two.start()
    place = in_slot(cp_v[...]).astype(BF16)
    self_two.wait()
    arrived(land_two.at[pl.ds(0, tiles - 1)], two_sem.at[1])
    stage_pair[...] = land_two[...].astype(I32).astype(F32)
    for source_of in range(2):
        tracer = face if source_of == 0 else 1 - face
        values = jnp.concatenate(
            [stage_pair[:, part // 2, part % 2, :] for part in range(3 * source_of, 3 * source_of + 3)],
            axis=1,
        )
        octave = values[:, 3 * LANES - 1 :]
        values = values * (jnp.exp2(0.25 * octave) * (1.0 / CODE))
        high = values.astype(BF16)
        low = (values - high.astype(F32)).astype(BF16)
        result = row_dot(high, place) + row_dot(low, place)
        out[tracer] = result[: 4 * LEV].reshape(LEV, 4, LANES)

    arrived(metas.at[pl.ds(0, 9)], meta_sem.at[0])
    arrived(own_adj.at[0], pair_sem.at[0])
    arrived(own_mis.at[0], pair_sem.at[2])
    arrived(land_one.at[0, pl.ds(0, tiles - 1)], one_sem.at[0])
    arrived(halo_adj, halo_sem.at[0])
    arrived(halo_edge, halo_sem.at[2])
    arrived(halo_mis, halo_sem.at[4])
    arrived(land_one.at[1], pass_sem.at[0])
    arrived(other, pair_sem.at[4])
    arrived(land_two.at[pl.ds(0, tiles - 1)], two_sem.at[0])


def per_device(
    fwd_tracers, fwd_kappa, send_order, recv_place, depth_levels, horiz_rate, adj_init, misfit,
    ctrl_send, ctrl_place,
):
    tiles = lax.axis_size("tile")
    anywhere = pl.BlockSpec(memory_space=pltpu.HBM)
    vmem = pltpu.VMEM
    dma = pltpu.SemaphoreType.DMA
    block = (LEV, 4, LANES)
    level_rows = (LEV, 3, 8, LANES)
    scratch = [
        pltpu.SMEM((LEV,), F32),
        vmem((2, LEV + 1, 4, LANES), BF16), vmem((LEV + 1, 4, LANES), BF16),
        vmem((1, LANES), I32), vmem((1, LANES), I32), vmem((4, LANES), I32),
        vmem((2,) + block, F32), vmem((2,) + block, F32),
        vmem((1, LANES), I32), vmem((1, LANES), I32),
        vmem((384, LANES), F32), vmem((tiles, 5, 2, LANES), F32),
        vmem((tiles, 5, 2, LANES), BF16), vmem((2, tiles, 5, 2, LANES), BF16),
        vmem((2, 8, LANES), I32), vmem((10, 2, 8, LANES), I32),
        vmem((2,) + block, BF16), vmem((2,) + block, BF16), vmem((2, 2, LEV // 2, 2, LANES), BF16),
        vmem((4,) + block, BF16), vmem((4,) + block, BF16), vmem((4, LEV // 2, 2, LANES), BF16),
        vmem((2,) + block, F32), vmem((2,) + block, F32),
        vmem((2, 3, 384, LANES), F32), vmem((LEV, 5, 8, LANES), F32),
        vmem(level_rows, F32), vmem(level_rows, F32), vmem(level_rows, F32),
        vmem(level_rows, F32), vmem(level_rows, F32),
        vmem((2, 384, LANES), F32), vmem((384, LANES), F32),
        vmem((tiles, 3, 2, LANES), I16), vmem((tiles, 3, 2, LANES), I16),
        vmem((tiles, 3, 2, LANES), F32),
        dma((14,)), dma((2,)), dma((2,)), dma((2,)), dma((6,)), dma((6,)), dma((2,)),
    ]
    return pl.pallas_call(
        functools.partial(kernel, tiles),
        out_shape=jax.ShapeDtypeStruct((2,) + block, F32),
        in_specs=[anywhere] * 10,
        out_specs=pl.BlockSpec(memory_space=pltpu.VMEM),
        scratch_shapes=scratch,
        compiler_params=pltpu.CompilerParams(
            collective_id=0, has_side_effects=True, vmem_limit_bytes=60 * 2**20
        ),
        cost_estimate=pl.CostEstimate(
            flops=10**9, bytes_accessed=4 * 2**20, transcendentals=10**5
        ),
    )(
        fwd_tracers, fwd_kappa, send_order, recv_place, depth_levels, horiz_rate, adj_init, misfit,
        ctrl_send, ctrl_place,
    )


def solution(mesh):
    placed = (
        P(None, None, None, ("face", "tile")),
        P(None, None, ("face", "tile")),
        P("face", "tile", None),
        P("face", "tile", None),
        P("tile", "face"),
        P(),
        P(None, None, "tile", "face"),
        P(None, None, "tile", "face"),
        P("face", "tile", None),
        P("face", "tile", None),
    )
    return jax.shard_map(
        per_device,
        mesh=mesh,
        in_specs=placed,
        out_specs=P(None, None, None, ("face", "tile")),
        check_vma=False,
    )
```

```python
import functools

import jax
import jax.numpy as jnp
from jax import lax
from jax.experimental import pallas as pl
from jax.experimental.pallas import tpu as pltpu
from jax.sharding import PartitionSpec as P

MESH = pl.DeviceIdType.MESH
F32 = jnp.float32
BF16 = jnp.bfloat16
I32 = jnp.int32
I16 = jnp.int16

LEV = 90
STEPS = 5
LANES = 128
UNROLL = 10
SWEEP = 90
CODE = 32000.0
SIDES = ((0, 1), (1, -1))


def ordered(slot, face0, face1):
    return (face0, face1) if slot % 2 == 0 else (face1, face0)


def stack_faces(slot, face0, face1):
    first, second = ordered(slot, face0, face1)
    return jnp.concatenate([first, second], axis=0)


def in_slot(index_array):
    rows = lax.broadcasted_iota(I32, (LANES, LANES), 0)
    return (rows == index_array).astype(F32)


def column_dot(lhs, rhs):
    return lax.dot_general(lhs, rhs, (((1,), (1,)), ((), ())), preferred_element_type=F32)


def row_dot(lhs, rhs):
    return lax.dot_general(lhs, rhs, (((0,), (1,)), ((), ())), preferred_element_type=F32)


def kernel(
    tiles,
    fwd, kap, send_order, recv_place, depth, rate_in, adj, mis, ctrl_send, ctrl_place,
    land_two,
    rate, fwd_v, kap_v, so_v, rp_v, depth_v, adj_v, mis_v, cs_v, cp_v,
    coup_v, stage, send_one, land_one,
    meta, metas, half_adj, half_mis, edge_adj, halo_adj, halo_mis, halo_edge, own_adj, own_mis,
    placed, give, take, state, middle, keep, factor, inverse, source,
    final, other, send_two, stage_pair,
    local, meta_sem, one_sem, pass_sem, halo_sem, pair_sem, two_sem,
):
    tile = lax.axis_index("tile")
    face = lax.axis_index("face")
    barrier = pltpu.get_barrier_semaphore()

    def to_tile(shift):
        return lax.rem(tile + (shift + tiles), tiles)

    def greet(step, carry):
        pl.semaphore_signal(
            barrier, inc=1, device_id=(face, lax.rem(tile + step, tiles)), device_id_type=MESH
        )
        return carry

    for shift in (-2, -1, 0, 1, 2):
        pl.semaphore_signal(
            barrier, inc=1, device_id=(1 - face, to_tile(shift)), device_id_type=MESH
        )
    lax.fori_loop(1, tiles, greet, 0)

    moves = [
        pltpu.make_async_copy(src, dst, local.at[i])
        for i, (src, dst) in enumerate((
            (fwd, fwd_v.at[:, pl.ds(0, LEV)]),
            (kap, kap_v.at[pl.ds(0, LEV)]),
            (send_order.at[0], so_v),
            (recv_place.at[0], rp_v),
            (depth, depth_v),
            (adj, adj_v),
            (mis, mis_v),
            (ctrl_send.at[0], cs_v),
            (ctrl_place.at[0], cp_v),
            (adj.at[face], own_adj.at[face]),
            (mis.at[face], own_mis.at[face]),
            (rate_in, rate),
        ))
    ]
    for move in moves:
        move.start()
    fwd_v[0, LEV] = jnp.zeros((4, LANES), BF16)
    fwd_v[1, LEV] = jnp.zeros((4, LANES), BF16)
    kap_v[LEV] = jnp.zeros((4, LANES), BF16)
    coup_v[pl.ds(4 * LEV, 24)] = jnp.zeros((24, LANES), F32)
    stage[:, 4, 1, :] = jnp.zeros((LANES, LANES), F32)

    for move in moves[:4]:
        move.wait()

    def density(level):
        return 0.8 * fwd_v[1, level].astype(F32) - 0.2 * fwd_v[0, level].astype(F32)

    def couple(block, carry):
        above, kappa_above = carry
        for pair in range(5):
            rows = []
            for half in range(2):
                level = block * 10 + pair * 2 + half + 1
                below = density(level)
                kappa_below = kap_v[level].astype(F32)
                contrast = below - above
                rows.append(
                    0.5 * (kappa_above + kappa_below) * (1.0 + 3.0 * jax.nn.sigmoid(-4.0 * contrast))
                )
                above, kappa_above = below, kappa_below
            coup_v[pl.ds(pl.multiple_of(block * 40 + pair * 8, 8), 8)] = jnp.concatenate(rows, axis=0)
        return above, kappa_above

    lax.fori_loop(0, LEV // 10, couple, (density(0), kap_v[0].astype(F32)))

    pick = in_slot(so_v[...]).T.astype(BF16)
    pieces = column_dot(pick, coup_v[...].astype(BF16))
    for beside in range(3):
        moved = pieces if beside == 1 else pltpu.roll(pieces, (1 - beside) % tiles, 0)
        for part in range(3):
            at = 3 * beside + part
            stage[:, at // 2, at % 2, :] = moved[:, part * LANES : (part + 1) * LANES]
    send_one[...] = stage[...].astype(BF16)

    moves[4].wait()
    meta[0] = jnp.concatenate([depth_v[...], depth_v[...]], axis=0)
    meta[1] = jnp.broadcast_to(rp_v[...], (8, LANES))
    metas[4 + face] = meta[...]
    moves[5].wait()
    for tracer in range(2):
        half_adj[tracer] = adj_v[tracer].astype(BF16)

    def outline(block, carry):
        for pair in range(3):
            level = 2 * (block * 3 + pair)
            for tracer in range(2):
                for side, line in ((0, 3), (1, 0)):
                    rows = [adj_v[tracer, level + half, line : line + 1, :] for half in range(2)]
                    edge_adj[side, tracer, block * 3 + pair] = jnp.concatenate(
                        rows, axis=0
                    ).astype(BF16)
        return carry

    lax.fori_loop(0, LEV // 6, outline, 0)
    moves[6].wait()
    for tracer in range(2):
        half_mis[tracer] = mis_v[tracer].astype(BF16)

    pl.semaphore_wait(barrier, tiles + 4)

    def remote(src, dst, send_sem, recv_sem, to_face, to):
        pltpu.make_async_remote_copy(
            src_ref=src, dst_ref=dst, send_sem=send_sem, recv_sem=recv_sem,
            device_id=(to_face, to), device_id_type=MESH,
        ).start()

    for shift in (-1, 1, -2, 2):
        for tracer in range(2):
            remote(
                meta, metas.at[2 * (2 - shift) + face],
                meta_sem.at[0], meta_sem.at[1], tracer, to_tile(shift),
            )
    remote(meta, metas.at[4 + face], meta_sem.at[0], meta_sem.at[1], 1 - face, tile)
    remote(
        adj.at[1 - face], own_adj.at[face], pair_sem.at[0], pair_sem.at[1], 1 - face, tile
    )
    remote(
        mis.at[1 - face], own_mis.at[face], pair_sem.at[2], pair_sem.at[3], 1 - face, tile
    )

    def route_one(step, carry):
        to = lax.rem(tile + step, tiles)
        remote(
            send_one.at[to], land_one.at[tile], one_sem.at[0], one_sem.at[1], face, to
        )
        return carry

    lax.fori_loop(1, tiles, route_one, 0)
    self_one = pltpu.make_async_copy(
        send_one.at[tile], land_one.at[tile], local.at[12]
    )
    self_one.start()
    for side, shift in SIDES:
        for tracer in range(2):
            remote(
                half_adj.at[tracer], halo_adj.at[2 * side + face],
                halo_sem.at[0], halo_sem.at[1], tracer, to_tile(shift),
            )
            remote(
                edge_adj.at[side, tracer], halo_edge.at[2 * side + face],
                halo_sem.at[2], halo_sem.at[3], tracer, to_tile(2 * shift),
            )
    for side, shift in SIDES:
        for tracer in range(2):
            remote(
                half_mis.at[tracer], halo_mis.at[2 * side + face],
                halo_sem.at[4], halo_sem.at[5], tracer, to_tile(shift),
            )

    def arrived(ref, semaphore):
        pltpu.make_async_copy(ref, ref, semaphore).wait()

    row = lax.broadcasted_iota(I32, (8, LANES), 0)
    lane = lax.broadcasted_iota(I32, (8, LANES), 1)
    cell = row % 4
    first_cell, last_cell = cell == 0, cell == 3
    first_lane, last_lane = lane == 0, lane == LANES - 1
    low_lane, low_row = lane < LANES // 2, row < 4
    seam_even = low_lane == low_row
    seam_odd = low_lane != low_row

    def neighbours(slot, west, here, east):
        seam = jnp.where(seam_even if slot % 2 == 0 else seam_odd, pltpu.roll(here, 4, 0), 0.0)
        return (
            pltpu.roll(jnp.where(first_cell, east, here), 7, 0),
            pltpu.roll(jnp.where(last_cell, west, here), 1, 0),
            pltpu.roll(jnp.where(first_lane, seam, here), LANES - 1, 1),
            pltpu.roll(jnp.where(last_lane, seam, here), 1, 1),
        )

    arrived(metas.at[pl.ds(0, 9)], meta_sem.at[1])
    depths = []
    for slot in range(5):
        at = tile + (slot - 2)
        inside = jnp.logical_and(at >= 0, at < tiles).astype(F32)
        first, second = ordered(slot, metas[2 * slot, 0], metas[2 * slot + 1, 0])
        depths.append(jnp.where(low_row, first, second).astype(F32) * inside)
    around = [
        neighbours(slot, depths[slot - 1], depths[slot], depths[slot + 1]) for slot in (1, 2, 3)
    ]

    def wet(level, slot):
        return level.astype(F32) < depths[slot]

    def prepare(block, carry):
        for inner in range(5):
            level = block * 5 + inner
            at = level.astype(F32)
            speed = rate[level]
            for slot in (1, 2, 3):
                count = jnp.zeros((8, LANES), F32)
                for beside in around[slot - 1]:
                    count = count + jnp.where(at < beside, 1.0, 0.0)
                keep[level, slot - 1] = 1.0 - speed * count
        return carry

    moves[11].wait()
    lax.fori_loop(0, LEV // 5, prepare, 0)

    self_one.wait()
    arrived(land_one.at[pl.ds(0, tiles - 1)], one_sem.at[1])
    stage[...] = land_one[...].astype(F32)
    for part in range(3):
        held = jnp.concatenate(
            [stage[:, at // 2, at % 2, :] for at in range(3 * part, 3 * part + 3)], axis=1
        ).astype(BF16)
        place = in_slot(metas[2 * (part + 1) + face, 1][0:1, :]).astype(BF16)
        result = row_dot(held, place)
        give[part] = result.astype(BF16)
        remote(
            give.at[part], take.at[part], pass_sem.at[part], pass_sem.at[3 + part], 1 - face, tile
        )
        placed[face, part] = result
    moves[9].wait()
    arrived(own_adj.at[0], pair_sem.at[1])
    arrived(halo_adj, halo_sem.at[1])
    arrived(halo_edge, halo_sem.at[3])

    def begin(block, carry):
        for inner in range(6):
            level = block * 6 + inner
            lines = [
                halo_edge[i, block * 3 + inner // 2].astype(F32)[inner % 2 : inner % 2 + 1]
                for i in range(4)
            ]
            tile_of = {
                1: stack_faces(1, halo_adj[0, level].astype(F32), halo_adj[1, level].astype(F32)),
                2: stack_faces(2, own_adj[0, level], own_adj[1, level]),
                3: stack_faces(3, halo_adj[2, level].astype(F32), halo_adj[3, level].astype(F32)),
                0: jnp.where(low_row, lines[0], lines[1]),
                4: jnp.where(low_row, lines[2], lines[3]),
            }
            for slot in range(5):
                state[level, slot] = jnp.where(wet(level, slot), tile_of[slot], 0.0)
        return carry

    lax.fori_loop(0, LEV // 6, begin, 0)
    for part in range(3):
        arrived(take.at[part], pass_sem.at[3 + part])
        placed[1 - face, part] = take[part].astype(F32)

    one = jnp.ones((8, LANES), F32)

    def eliminate(block, carry):
        carry = [(upper / lower, one) for upper, lower in carry]
        for pair in range(UNROLL // 2):
            base = pl.multiple_of(block * (4 * UNROLL) + pair * 8, 8)
            for slot in (1, 2, 3):
                first, second = ordered(
                    slot, placed[0, slot - 1, pl.ds(base, 8)], placed[1, slot - 1, pl.ds(base, 8)]
                )
                couplings = (
                    jnp.where(low_row, first, pltpu.roll(second, 4, 0)),
                    jnp.where(low_row, pltpu.roll(first, 4, 0), second),
                )
                upper, lower = carry[slot - 1]
                for half in range(2):
                    level = block * UNROLL + pair * 2 + half
                    weight = jnp.where(
                        (level + 1).astype(F32) < depths[slot], couplings[half], 0.0
                    )
                    next_lower = upper + weight * lower
                    next_upper = next_lower + weight * upper
                    ratio = lower / next_lower
                    factor[level, slot - 1] = weight * ratio
                    inverse[level, slot - 1] = jnp.where(wet(level, slot), ratio, 0.0)
                    upper, lower = next_upper, next_lower
                carry[slot - 1] = (upper, lower)
        return carry

    lax.fori_loop(0, LEV // UNROLL, eliminate, [(one, one)] * 3)

    zero = jnp.zeros((8, LANES), F32)

    def descend(slots, block, carry):
        carry = list(carry)
        for inner in range(SWEEP):
            level = block * SWEEP + inner
            speed = rate[level]
            tile_of = {
                slot: state[level, slot] for slot in range(slots[0] - 1, slots[-1] + 2)
            }
            for i, slot in enumerate(slots):
                east, west, north, south = neighbours(
                    slot, tile_of[slot - 1], tile_of[slot], tile_of[slot + 1]
                )
                spread = keep[level, slot - 1] * tile_of[slot] + speed * (
                    (east + west) + (north + south)
                )
                value = spread + carry[i]
                middle[level, slot - 1] = value
                carry[i] = factor[level, slot - 1] * value
        return carry

    def ascend(slots, last, block, carry):
        carry = list(carry)
        for pair in range(SWEEP // 2):
            halves = []
            for inner in range(2):
                level = (LEV - 1) - (block * SWEEP + pair * 2 + inner)
                for i, slot in enumerate(slots):
                    solved = (
                        middle[level, slot - 1] * inverse[level, slot - 1]
                        + factor[level, slot - 1] * carry[i]
                    )
                    carry[i] = solved
                    value = solved + source[level, slot - 1]
                    if last:
                        halves.append(value)
                    else:
                        state[level, slot] = value
            if last:
                below, above = halves
                base = pl.multiple_of(
                    (4 * LEV - 8) - (block * (4 * SWEEP) + pair * 8), 8
                )
                final[0, pl.ds(base, 8)] = jnp.where(low_row, above, pltpu.roll(below, 4, 0))
                final[1, pl.ds(base, 8)] = jnp.where(low_row, pltpu.roll(above, 4, 0), below)
        return carry

    def advance(step, carry):
        lax.fori_loop(0, LEV // SWEEP, functools.partial(descend, (1, 2, 3)), [zero] * 3)
        lax.fori_loop(0, LEV // SWEEP, functools.partial(ascend, (1, 2, 3), False), [zero] * 3)
        return carry

    sweep_down = functools.partial(descend, (1, 2, 3))
    lax.fori_loop(0, LEV // SWEEP, sweep_down, [zero] * 3)
    moves[10].wait()
    arrived(own_mis.at[0], pair_sem.at[3])
    arrived(halo_mis, halo_sem.at[5])

    def drive(block, carry):
        for inner in range(5):
            level = block * 5 + inner
            tile_of = {
                1: stack_faces(1, halo_mis[0, level].astype(F32), halo_mis[1, level].astype(F32)),
                2: stack_faces(2, own_mis[0, level], own_mis[1, level]),
                3: stack_faces(3, halo_mis[2, level].astype(F32), halo_mis[3, level].astype(F32)),
            }
            for slot in (1, 2, 3):
                source[level, slot - 1] = jnp.where(wet(level, slot), tile_of[slot], 0.0)
        return carry

    lax.fori_loop(0, LEV // 5, drive, 0)

    lax.fori_loop(0, LEV // SWEEP, functools.partial(ascend, (1, 2, 3), False), [zero] * 3)
    lax.fori_loop(1, STEPS - 1, advance, 0)
    lax.fori_loop(0, LEV // SWEEP, functools.partial(descend, (2,)), [zero])
    final[0, pl.ds(4 * LEV, 24)] = jnp.zeros((24, LANES), F32)
    final[1, pl.ds(4 * LEV, 24)] = jnp.zeros((24, LANES), F32)
    lax.fori_loop(0, LEV // SWEEP, functools.partial(ascend, (2,), True), [zero])

    remote(final.at[1 - face], other, pair_sem.at[4], pair_sem.at[5], 1 - face, tile)
    moves[7].wait()
    moves[8].wait()
    choose = in_slot(cs_v[...]).T.astype(BF16)
    end_lane = lax.broadcasted_iota(I32, (LANES, LANES), 1) == LANES - 1
    for source_of in range(2):
        if source_of == 0:
            values = final[face]
        else:
            arrived(other, pair_sem.at[5])
            values = other[...]
        high = values.astype(BF16)
        low = (values - high.astype(F32)).astype(BF16)
        pieces = column_dot(choose, high) + column_dot(choose, low)
        largest = jnp.max(jnp.abs(pieces), axis=1, keepdims=True)
        octave = jnp.ceil(4.0 * jnp.log2(jnp.maximum(largest, 1e-33)) + 0.01)
        codes = jnp.floor(pieces * (CODE / jnp.exp2(0.25 * octave)) + 0.5)
        for part in range(3):
            column = codes[:, part * LANES : (part + 1) * LANES]
            if part == 2:
                column = jnp.where(end_lane, octave, column)
            stage_pair[:, (3 * source_of + part) // 2, (3 * source_of + part) % 2, :] = column
    send_two[...] = stage_pair[...].astype(I32).astype(I16)

    def route_two(step, carry):
        to = lax.rem(tile + step, tiles)
        remote(send_two.at[to], land_two.at[tile], two_sem.at[0], two_sem.at[1], face, to)
        return carry

    lax.fori_loop(1, tiles, route_two, 0)
    self_two = pltpu.make_async_copy(send_two.at[tile], land_two.at[tile], local.at[13])
    self_two.start()
    self_two.wait()
    arrived(land_two.at[pl.ds(0, tiles - 1)], two_sem.at[1])

    arrived(metas.at[pl.ds(0, 9)], meta_sem.at[0])
    arrived(own_adj.at[0], pair_sem.at[0])
    arrived(own_mis.at[0], pair_sem.at[2])
    arrived(land_one.at[pl.ds(0, tiles - 1)], one_sem.at[0])
    arrived(halo_adj, halo_sem.at[0])
    arrived(halo_edge, halo_sem.at[2])
    arrived(halo_mis, halo_sem.at[4])
    for part in range(3):
        arrived(give.at[part], pass_sem.at[part])
    arrived(other, pair_sem.at[4])
    arrived(land_two.at[pl.ds(0, tiles - 1)], two_sem.at[0])


def deliver(land_two, cp_v, out, stage_pair):
    face = lax.axis_index("face")
    place = in_slot(cp_v[0]).astype(BF16)
    stage_pair[...] = land_two[...].astype(I32).astype(F32)
    for source_of in range(2):
        tracer = face if source_of == 0 else 1 - face
        values = jnp.concatenate(
            [stage_pair[:, part // 2, part % 2, :] for part in range(3 * source_of, 3 * source_of + 3)],
            axis=1,
        )
        octave = values[:, 3 * LANES - 1 :]
        values = values * (jnp.exp2(0.25 * octave) * (1.0 / CODE))
        high = values.astype(BF16)
        low = (values - high.astype(F32)).astype(BF16)
        result = row_dot(high, place) + row_dot(low, place)
        out[tracer] = result[: 4 * LEV].reshape(LEV, 4, LANES)


def per_device(
    fwd_tracers, fwd_kappa, send_order, recv_place, depth_levels, horiz_rate, adj_init, misfit,
    ctrl_send, ctrl_place,
):
    tiles = lax.axis_size("tile")
    anywhere = pl.BlockSpec(memory_space=pltpu.HBM)
    vmem = pltpu.VMEM
    dma = pltpu.SemaphoreType.DMA
    block = (LEV, 4, LANES)
    level_rows = (LEV, 3, 8, LANES)
    scratch = [
        pltpu.SMEM((LEV,), F32),
        vmem((2, LEV + 1, 4, LANES), BF16), vmem((LEV + 1, 4, LANES), BF16),
        vmem((1, LANES), I32), vmem((1, LANES), I32), vmem((4, LANES), I32),
        vmem((2,) + block, F32), vmem((2,) + block, F32),
        vmem((1, LANES), I32), vmem((1, LANES), I32),
        vmem((384, LANES), F32), vmem((tiles, 5, 2, LANES), F32),
        vmem((tiles, 5, 2, LANES), BF16), vmem((tiles, 5, 2, LANES), BF16),
        vmem((2, 8, LANES), I32), vmem((10, 2, 8, LANES), I32),
        vmem((2,) + block, BF16), vmem((2,) + block, BF16), vmem((2, 2, LEV // 2, 2, LANES), BF16),
        vmem((4,) + block, BF16), vmem((4,) + block, BF16), vmem((4, LEV // 2, 2, LANES), BF16),
        vmem((2,) + block, F32), vmem((2,) + block, F32),
        vmem((2, 3, 384, LANES), F32), vmem((3, 384, LANES), BF16), vmem((3, 384, LANES), BF16),
        vmem((LEV, 5, 8, LANES), F32),
        vmem(level_rows, F32), vmem(level_rows, F32), vmem(level_rows, F32),
        vmem(level_rows, F32), vmem(level_rows, F32),
        vmem((2, 384, LANES), F32), vmem((384, LANES), F32),
        vmem((tiles, 3, 2, LANES), I16),
        vmem((tiles, 3, 2, LANES), F32),
        dma((14,)), dma((2,)), dma((2,)), dma((6,)), dma((6,)), dma((6,)), dma((2,)),
    ]
    landed = pl.pallas_call(
        functools.partial(kernel, tiles),
        out_shape=jax.ShapeDtypeStruct((tiles, 3, 2, LANES), I16),
        in_specs=[anywhere] * 10,
        out_specs=pl.BlockSpec(memory_space=pl.ANY),
        scratch_shapes=scratch,
        compiler_params=pltpu.CompilerParams(
            collective_id=0, has_side_effects=True, vmem_limit_bytes=60 * 2**20
        ),
        cost_estimate=pl.CostEstimate(
            flops=10**9, bytes_accessed=4 * 2**20, transcendentals=10**5
        ),
    )(
        fwd_tracers, fwd_kappa, send_order, recv_place, depth_levels, horiz_rate, adj_init, misfit,
        ctrl_send, ctrl_place,
    )
    return pl.pallas_call(
        deliver,
        out_shape=jax.ShapeDtypeStruct((2,) + block, F32),
        in_specs=[pl.BlockSpec(memory_space=pltpu.VMEM)] * 2,
        out_specs=pl.BlockSpec(memory_space=pltpu.VMEM),
        scratch_shapes=[vmem((tiles, 3, 2, LANES), F32)],
        compiler_params=pltpu.CompilerParams(vmem_limit_bytes=60 * 2**20),
    )(landed, ctrl_place)


def solution(mesh):
    placed = (
        P(None, None, None, ("face", "tile")),
        P(None, None, ("face", "tile")),
        P("face", "tile", None),
        P("face", "tile", None),
        P("tile", "face"),
        P(),
        P(None, None, "tile", "face"),
        P(None, None, "tile", "face"),
        P("face", "tile", None),
        P("face", "tile", None),
    )
    return jax.shard_map(
        per_device,
        mesh=mesh,
        in_specs=placed,
        out_specs=P(None, None, None, ("face", "tile")),
        check_vma=False,
    )
```

```python
import functools

import jax
import jax.numpy as jnp
from jax import lax
from jax.experimental import pallas as pl
from jax.experimental.pallas import tpu as pltpu
from jax.sharding import PartitionSpec as P

MESH = pl.DeviceIdType.MESH
F32 = jnp.float32
BF16 = jnp.bfloat16
I32 = jnp.int32
I16 = jnp.int16

LEV = 90
STEPS = 5
LANES = 128
UNROLL = 10
CODE = 32000.0
SIDES = ((0, 1), (1, -1))


def ordered(slot, face0, face1):
    return (face0, face1) if slot % 2 == 0 else (face1, face0)


def stack_faces(slot, face0, face1):
    first, second = ordered(slot, face0, face1)
    return jnp.concatenate([first, second], axis=0)


def in_slot(index_array):
    rows = lax.broadcasted_iota(I32, (LANES, LANES), 0)
    return (rows == index_array).astype(F32)


def column_dot(lhs, rhs):
    return lax.dot_general(lhs, rhs, (((1,), (1,)), ((), ())), preferred_element_type=F32)


def row_dot(lhs, rhs):
    return lax.dot_general(lhs, rhs, (((0,), (1,)), ((), ())), preferred_element_type=F32)


def kernel(
    tiles,
    fwd, kap, send_order, recv_place, depth, rate_in, adj, mis, ctrl_send, ctrl_place,
    land_two,
    rate, fwd_v, kap_v, so_v, rp_v, depth_v, adj_v, mis_v, cs_v, cp_v,
    coup_v, stage, send_one, land_one,
    meta, metas, half_adj, half_mis, edge_adj, halo_adj, halo_mis, halo_edge, own_adj, own_mis,
    places, placed, give, take, state, middle, keep, factor, inverse, source,
    final, other, send_two, stage_pair,
    local, meta_sem, one_sem, pass_sem, halo_sem, pair_sem, two_sem,
):
    tile = lax.axis_index("tile")
    face = lax.axis_index("face")
    barrier = pltpu.get_barrier_semaphore()

    def to_tile(shift):
        return lax.rem(tile + (shift + tiles), tiles)

    def greet(step, carry):
        pl.semaphore_signal(
            barrier, inc=1, device_id=(face, lax.rem(tile + step, tiles)), device_id_type=MESH
        )
        return carry

    for shift in (-2, -1, 0, 1, 2):
        pl.semaphore_signal(
            barrier, inc=1, device_id=(1 - face, to_tile(shift)), device_id_type=MESH
        )
    lax.fori_loop(1, tiles, greet, 0)

    moves = [
        pltpu.make_async_copy(src, dst, local.at[i])
        for i, (src, dst) in enumerate((
            (fwd, fwd_v.at[:, pl.ds(0, LEV)]),
            (kap, kap_v.at[pl.ds(0, LEV)]),
            (send_order.at[0], so_v),
            (recv_place.at[0], rp_v),
            (depth, depth_v),
            (adj, adj_v),
            (mis, mis_v),
            (ctrl_send.at[0], cs_v),
            (ctrl_place.at[0], cp_v),
            (adj.at[face], own_adj.at[face]),
            (mis.at[face], own_mis.at[face]),
            (rate_in, rate),
        ))
    ]
    for move in moves:
        move.start()
    fwd_v[0, LEV] = jnp.zeros((4, LANES), BF16)
    fwd_v[1, LEV] = jnp.zeros((4, LANES), BF16)
    kap_v[LEV] = jnp.zeros((4, LANES), BF16)
    coup_v[pl.ds(4 * LEV, 24)] = jnp.zeros((24, LANES), F32)
    stage[:, 4, 1, :] = jnp.zeros((LANES, LANES), F32)

    for move in moves[:4]:
        move.wait()

    def density(level):
        return 0.8 * fwd_v[1, level].astype(F32) - 0.2 * fwd_v[0, level].astype(F32)

    def couple(block, carry):
        above, kappa_above = carry
        for pair in range(5):
            rows = []
            for half in range(2):
                level = block * 10 + pair * 2 + half + 1
                below = density(level)
                kappa_below = kap_v[level].astype(F32)
                contrast = below - above
                rows.append(
                    0.5 * (kappa_above + kappa_below) * (1.0 + 3.0 * jax.nn.sigmoid(-4.0 * contrast))
                )
                above, kappa_above = below, kappa_below
            coup_v[pl.ds(pl.multiple_of(block * 40 + pair * 8, 8), 8)] = jnp.concatenate(rows, axis=0)
        return above, kappa_above

    lax.fori_loop(0, LEV // 10, couple, (density(0), kap_v[0].astype(F32)))

    pick = in_slot(so_v[...]).T.astype(BF16)
    pieces = column_dot(pick, coup_v[...].astype(BF16))
    for beside in range(3):
        moved = pieces if beside == 1 else pltpu.roll(pieces, (1 - beside) % tiles, 0)
        for part in range(3):
            at = 3 * beside + part
            stage[:, at // 2, at % 2, :] = moved[:, part * LANES : (part + 1) * LANES]
    send_one[...] = stage[...].astype(BF16)

    moves[4].wait()
    meta[0] = jnp.concatenate([depth_v[...], depth_v[...]], axis=0)
    meta[1] = jnp.broadcast_to(rp_v[...], (8, LANES))
    metas[4 + face] = meta[...]
    moves[5].wait()
    for tracer in range(2):
        half_adj[tracer] = adj_v[tracer].astype(BF16)

    def outline(block, carry):
        for pair in range(3):
            level = 2 * (block * 3 + pair)
            for tracer in range(2):
                for side, line in ((0, 3), (1, 0)):
                    rows = [adj_v[tracer, level + half, line : line + 1, :] for half in range(2)]
                    edge_adj[side, tracer, block * 3 + pair] = jnp.concatenate(
                        rows, axis=0
                    ).astype(BF16)
        return carry

    lax.fori_loop(0, LEV // 6, outline, 0)
    moves[6].wait()
    for tracer in range(2):
        half_mis[tracer] = mis_v[tracer].astype(BF16)

    pl.semaphore_wait(barrier, tiles + 4)

    def remote(src, dst, send_sem, recv_sem, to_face, to):
        pltpu.make_async_remote_copy(
            src_ref=src, dst_ref=dst, send_sem=send_sem, recv_sem=recv_sem,
            device_id=(to_face, to), device_id_type=MESH,
        ).start()

    for shift in (-1, 1, -2, 2):
        for tracer in range(2):
            remote(
                meta, metas.at[2 * (2 - shift) + face],
                meta_sem.at[0], meta_sem.at[1], tracer, to_tile(shift),
            )
    remote(meta, metas.at[4 + face], meta_sem.at[0], meta_sem.at[1], 1 - face, tile)
    remote(
        adj.at[1 - face], own_adj.at[face], pair_sem.at[0], pair_sem.at[1], 1 - face, tile
    )
    remote(
        mis.at[1 - face], own_mis.at[face], pair_sem.at[2], pair_sem.at[3], 1 - face, tile
    )

    def route_one(step, carry):
        to = lax.rem(tile + step, tiles)
        remote(
            send_one.at[to], land_one.at[tile], one_sem.at[0], one_sem.at[1], face, to
        )
        return carry

    lax.fori_loop(1, tiles, route_one, 0)
    self_one = pltpu.make_async_copy(
        send_one.at[tile], land_one.at[tile], local.at[12]
    )
    self_one.start()
    for side, shift in SIDES:
        for tracer in range(2):
            remote(
                half_adj.at[tracer], halo_adj.at[2 * side + face],
                halo_sem.at[0], halo_sem.at[1], tracer, to_tile(shift),
            )
            remote(
                edge_adj.at[side, tracer], halo_edge.at[2 * side + face],
                halo_sem.at[2], halo_sem.at[3], tracer, to_tile(2 * shift),
            )
    for side, shift in SIDES:
        for tracer in range(2):
            remote(
                half_mis.at[tracer], halo_mis.at[2 * side + face],
                halo_sem.at[4], halo_sem.at[5], tracer, to_tile(shift),
            )

    def arrived(ref, semaphore):
        pltpu.make_async_copy(ref, ref, semaphore).wait()

    row = lax.broadcasted_iota(I32, (8, LANES), 0)
    lane = lax.broadcasted_iota(I32, (8, LANES), 1)
    cell = row % 4
    first_cell, last_cell = cell == 0, cell == 3
    first_lane, last_lane = lane == 0, lane == LANES - 1
    low_lane, low_row = lane < LANES // 2, row < 4
    east_wing = cell < 2
    seam_even = low_lane == low_row
    seam_odd = low_lane != low_row

    def neighbours(slot, west, here, east, to_west=None, to_east=None):
        to_west = here if to_west is None else to_west
        to_east = here if to_east is None else to_east
        seam = jnp.where(seam_even if slot % 2 == 0 else seam_odd, pltpu.roll(here, 4, 0), 0.0)
        return (
            pltpu.roll(jnp.where(first_cell, east, to_east), 7, 0),
            pltpu.roll(jnp.where(last_cell, west, to_west), 1, 0),
            pltpu.roll(jnp.where(first_lane, seam, here), LANES - 1, 1),
            pltpu.roll(jnp.where(last_lane, seam, here), 1, 1),
        )

    arrived(metas.at[pl.ds(0, 9)], meta_sem.at[1])
    depths = []
    for slot in range(5):
        at = tile + (slot - 2)
        inside = jnp.logical_and(at >= 0, at < tiles).astype(F32)
        first, second = ordered(slot, metas[2 * slot, 0], metas[2 * slot + 1, 0])
        depths.append(jnp.where(low_row, first, second).astype(F32) * inside)
    around = [
        neighbours(slot, depths[slot - 1], depths[slot], depths[slot + 1]) for slot in (1, 2, 3)
    ]

    def wet(level, slot):
        return level.astype(F32) < depths[slot]

    def store_wing(ref, level, values):
        for i in range(3):
            ref[level, i] = values[i]
        ref[level, 3] = jnp.where(east_wing, values[2], values[0])

    def prepare(block, carry):
        for inner in range(5):
            level = block * 5 + inner
            at = level.astype(F32)
            speed = rate[level]
            kept = []
            for slot in (1, 2, 3):
                count = jnp.zeros((8, LANES), F32)
                for beside in around[slot - 1]:
                    count = count + jnp.where(at < beside, 1.0, 0.0)
                kept.append(1.0 - speed * count)
            store_wing(keep, level, kept)
        return carry

    for part in range(3):
        places[part] = in_slot(metas[2 * (part + 1) + face, 1][0:1, :]).astype(BF16)
    moves[11].wait()
    lax.fori_loop(0, LEV // 5, prepare, 0)

    self_one.wait()
    arrived(land_one.at[pl.ds(0, tiles - 1)], one_sem.at[1])
    stage[...] = land_one[...].astype(F32)
    for part in range(3):
        held = jnp.concatenate(
            [stage[:, at // 2, at % 2, :] for at in range(3 * part, 3 * part + 3)], axis=1
        ).astype(BF16)
        result = row_dot(held, places[part])
        give[part] = result.astype(BF16)
        remote(
            give.at[part], take.at[part], pass_sem.at[part], pass_sem.at[3 + part], 1 - face, tile
        )
        placed[face, part] = result
    moves[9].wait()
    arrived(own_adj.at[0], pair_sem.at[1])
    arrived(halo_adj, halo_sem.at[1])
    arrived(halo_edge, halo_sem.at[3])

    def begin(block, carry):
        for inner in range(6):
            level = block * 6 + inner
            lines = [
                halo_edge[i, block * 3 + inner // 2].astype(F32)[inner % 2 : inner % 2 + 1]
                for i in range(4)
            ]
            tile_of = {
                1: stack_faces(1, halo_adj[0, level].astype(F32), halo_adj[1, level].astype(F32)),
                2: stack_faces(2, own_adj[0, level], own_adj[1, level]),
                3: stack_faces(3, halo_adj[2, level].astype(F32), halo_adj[3, level].astype(F32)),
                0: jnp.where(low_row, lines[0], lines[1]),
                4: jnp.where(low_row, lines[2], lines[3]),
            }
            for slot in range(5):
                state[level, slot] = jnp.where(wet(level, slot), tile_of[slot], 0.0)
        return carry

    lax.fori_loop(0, LEV // 6, begin, 0)
    for part in range(3):
        arrived(take.at[part], pass_sem.at[3 + part])
        placed[1 - face, part] = take[part].astype(F32)

    one = jnp.ones((8, LANES), F32)

    def eliminate(block, carry):
        carry = [(upper / lower, one) for upper, lower in carry]
        for pair in range(UNROLL // 2):
            base = pl.multiple_of(block * (4 * UNROLL) + pair * 8, 8)
            factors, inverses = ([], []), ([], [])
            for slot in (1, 2, 3):
                first, second = ordered(
                    slot, placed[0, slot - 1, pl.ds(base, 8)], placed[1, slot - 1, pl.ds(base, 8)]
                )
                couplings = (
                    jnp.where(low_row, first, pltpu.roll(second, 4, 0)),
                    jnp.where(low_row, pltpu.roll(first, 4, 0), second),
                )
                upper, lower = carry[slot - 1]
                for half in range(2):
                    level = block * UNROLL + pair * 2 + half
                    weight = jnp.where(
                        (level + 1).astype(F32) < depths[slot], couplings[half], 0.0
                    )
                    next_lower = upper + weight * lower
                    next_upper = next_lower + weight * upper
                    ratio = lower / next_lower
                    factors[half].append(weight * ratio)
                    inverses[half].append(jnp.where(wet(level, slot), ratio, 0.0))
                    upper, lower = next_upper, next_lower
                carry[slot - 1] = (upper, lower)
            for half in range(2):
                level = block * UNROLL + pair * 2 + half
                store_wing(factor, level, factors[half])
                store_wing(inverse, level, inverses[half])
        return carry

    lax.fori_loop(0, LEV // UNROLL, eliminate, [(one, one)] * 3)

    zero = jnp.zeros((8, LANES), F32)

    def across(slots, folding, level):
        held = {
            slot: state[level, slot]
            for slot in ((0, 1, 2, 3, 4) if 1 in slots else (1, 2, 3) if folding else (2, 5))
        }
        if 1 in slots:
            return [(held[slot], neighbours(slot, held[slot - 1], held[slot], held[slot + 1])) for slot in slots]
        here = held[2]
        if folding:
            west, east = held[1], held[3]
            wing = jnp.where(east_wing, east, west)
            to_east = jnp.where(last_cell, west, east)
            to_west = jnp.where(first_cell, east, west)
        else:
            west = east = wing = to_east = to_west = held[5]
        found = [(here, neighbours(2, west, here, east))]
        if 5 in slots:
            found.append((wing, neighbours(5, here, wing, here, to_west, to_east)))
        return found

    def descend(slots, folding=False):
        carry = [zero] * len(slots)
        for level in range(LEV):
            speed = rate[level]
            for i, (here, (east, west, north, south)) in enumerate(across(slots, folding, level)):
                at = slots[i] - 1 if slots[i] < 5 else 3
                value = (
                    keep[level, at] * here + speed * ((east + west) + (north + south)) + carry[i]
                )
                middle[level, at] = value
                carry[i] = factor[level, at] * value

    def ascend(slots, last=False):
        carry = [zero] * len(slots)
        for pair in range(LEV // 2):
            halves = []
            for inner in range(2):
                level = LEV - 1 - (2 * pair + inner)
                for i, slot in enumerate(slots):
                    at = slot - 1 if slot < 5 else 3
                    solved = middle[level, at] * inverse[level, at] + factor[level, at] * carry[i]
                    carry[i] = solved
                    value = solved + source[level, at]
                    if last:
                        halves.append(value)
                    else:
                        state[level, slot] = value
            if last:
                below, above = halves
                base = 4 * LEV - 8 - 8 * pair
                final[0, pl.ds(base, 8)] = jnp.where(low_row, above, pltpu.roll(below, 4, 0))
                final[1, pl.ds(base, 8)] = jnp.where(low_row, pltpu.roll(above, 4, 0), below)

    descend((1, 2, 3))
    moves[10].wait()
    arrived(own_mis.at[0], pair_sem.at[3])
    arrived(halo_mis, halo_sem.at[5])

    def drive(block, carry):
        for inner in range(5):
            level = block * 5 + inner
            tile_of = {
                1: stack_faces(1, halo_mis[0, level].astype(F32), halo_mis[1, level].astype(F32)),
                2: stack_faces(2, own_mis[0, level], own_mis[1, level]),
                3: stack_faces(3, halo_mis[2, level].astype(F32), halo_mis[3, level].astype(F32)),
            }
            store_wing(
                source, level,
                [jnp.where(wet(level, slot), tile_of[slot], 0.0) for slot in (1, 2, 3)],
            )
        return carry

    lax.fori_loop(0, LEV // 5, drive, 0)

    ascend((1, 2, 3))
    descend((1, 2, 3))
    ascend((1, 2, 3))
    descend((2, 5), folding=True)
    ascend((2, 5))
    for step in range(3, STEPS - 1):
        descend((2, 5))
        ascend((2, 5))
    final[0, pl.ds(4 * LEV, 24)] = jnp.zeros((24, LANES), F32)
    final[1, pl.ds(4 * LEV, 24)] = jnp.zeros((24, LANES), F32)
    descend((2,))
    ascend((2,), last=True)

    remote(final.at[1 - face], other, pair_sem.at[4], pair_sem.at[5], 1 - face, tile)
    moves[7].wait()
    moves[8].wait()
    choose = in_slot(cs_v[...]).T.astype(BF16)
    end_lane = lax.broadcasted_iota(I32, (LANES, LANES), 1) == LANES - 1
    for source_of in range(2):
        if source_of == 0:
            values = final[face]
        else:
            arrived(other, pair_sem.at[5])
            values = other[...]
        high = values.astype(BF16)
        low = (values - high.astype(F32)).astype(BF16)
        pieces = column_dot(choose, high) + column_dot(choose, low)
        largest = jnp.max(jnp.abs(pieces), axis=1, keepdims=True)
        octave = jnp.ceil(4.0 * jnp.log2(jnp.maximum(largest, 1e-33)) + 0.01)
        codes = jnp.floor(pieces * (CODE / jnp.exp2(0.25 * octave)) + 0.5)
        for part in range(3):
            column = codes[:, part * LANES : (part + 1) * LANES]
            if part == 2:
                column = jnp.where(end_lane, octave, column)
            stage_pair[:, (3 * source_of + part) // 2, (3 * source_of + part) % 2, :] = column
    send_two[...] = stage_pair[...].astype(I32).astype(I16)

    def route_two(step, carry):
        to = lax.rem(tile + step, tiles)
        remote(send_two.at[to], land_two.at[tile], two_sem.at[0], two_sem.at[1], face, to)
        return carry

    lax.fori_loop(1, tiles, route_two, 0)
    self_two = pltpu.make_async_copy(send_two.at[tile], land_two.at[tile], local.at[13])
    self_two.start()
    self_two.wait()
    arrived(land_two.at[pl.ds(0, tiles - 1)], two_sem.at[1])

    arrived(metas.at[pl.ds(0, 9)], meta_sem.at[0])
    arrived(own_adj.at[0], pair_sem.at[0])
    arrived(own_mis.at[0], pair_sem.at[2])
    arrived(land_one.at[pl.ds(0, tiles - 1)], one_sem.at[0])
    arrived(halo_adj, halo_sem.at[0])
    arrived(halo_edge, halo_sem.at[2])
    arrived(halo_mis, halo_sem.at[4])
    for part in range(3):
        arrived(give.at[part], pass_sem.at[part])
    arrived(other, pair_sem.at[4])
    arrived(land_two.at[pl.ds(0, tiles - 1)], two_sem.at[0])


def deliver(land_two, cp_v, out, stage_pair):
    face = lax.axis_index("face")
    place = in_slot(cp_v[0]).astype(BF16)
    stage_pair[...] = land_two[...].astype(I32).astype(F32)
    for source_of in range(2):
        tracer = face if source_of == 0 else 1 - face
        values = jnp.concatenate(
            [stage_pair[:, part // 2, part % 2, :] for part in range(3 * source_of, 3 * source_of + 3)],
            axis=1,
        )
        octave = values[:, 3 * LANES - 1 :]
        values = values * (jnp.exp2(0.25 * octave) * (1.0 / CODE))
        high = values.astype(BF16)
        low = (values - high.astype(F32)).astype(BF16)
        result = row_dot(high, place) + row_dot(low, place)
        out[tracer] = result[: 4 * LEV].reshape(LEV, 4, LANES)


def per_device(
    fwd_tracers, fwd_kappa, send_order, recv_place, depth_levels, horiz_rate, adj_init, misfit,
    ctrl_send, ctrl_place,
):
    tiles = lax.axis_size("tile")
    anywhere = pl.BlockSpec(memory_space=pltpu.HBM)
    vmem = pltpu.VMEM
    dma = pltpu.SemaphoreType.DMA
    block = (LEV, 4, LANES)
    level_rows = (LEV, 4, 8, LANES)
    scratch = [
        pltpu.SMEM((LEV,), F32),
        vmem((2, LEV + 1, 4, LANES), BF16), vmem((LEV + 1, 4, LANES), BF16),
        vmem((1, LANES), I32), vmem((1, LANES), I32), vmem((4, LANES), I32),
        vmem((2,) + block, F32), vmem((2,) + block, F32),
        vmem((1, LANES), I32), vmem((1, LANES), I32),
        vmem((384, LANES), F32), vmem((tiles, 5, 2, LANES), F32),
        vmem((tiles, 5, 2, LANES), BF16), vmem((tiles, 5, 2, LANES), BF16),
        vmem((2, 8, LANES), I32), vmem((10, 2, 8, LANES), I32),
        vmem((2,) + block, BF16), vmem((2,) + block, BF16), vmem((2, 2, LEV // 2, 2, LANES), BF16),
        vmem((4,) + block, BF16), vmem((4,) + block, BF16), vmem((4, LEV // 2, 2, LANES), BF16),
        vmem((2,) + block, F32), vmem((2,) + block, F32),
        vmem((3, LANES, LANES), BF16),
        vmem((2, 3, 384, LANES), F32), vmem((3, 384, LANES), BF16), vmem((3, 384, LANES), BF16),
        vmem((LEV, 6, 8, LANES), F32),
        vmem(level_rows, F32), vmem(level_rows, F32), vmem(level_rows, F32),
        vmem(level_rows, F32), vmem(level_rows, F32),
        vmem((2, 384, LANES), F32), vmem((384, LANES), F32),
        vmem((tiles, 3, 2, LANES), I16),
        vmem((tiles, 3, 2, LANES), F32),
        dma((14,)), dma((2,)), dma((2,)), dma((6,)), dma((6,)), dma((6,)), dma((2,)),
    ]
    landed = pl.pallas_call(
        functools.partial(kernel, tiles),
        out_shape=jax.ShapeDtypeStruct((tiles, 3, 2, LANES), I16),
        in_specs=[anywhere] * 10,
        out_specs=pl.BlockSpec(memory_space=pl.ANY),
        scratch_shapes=scratch,
        compiler_params=pltpu.CompilerParams(
            collective_id=0, has_side_effects=True, vmem_limit_bytes=60 * 2**20
        ),
        cost_estimate=pl.CostEstimate(
            flops=10**9, bytes_accessed=4 * 2**20, transcendentals=10**5
        ),
    )(
        fwd_tracers, fwd_kappa, send_order, recv_place, depth_levels, horiz_rate, adj_init, misfit,
        ctrl_send, ctrl_place,
    )
    return pl.pallas_call(
        deliver,
        out_shape=jax.ShapeDtypeStruct((2,) + block, F32),
        in_specs=[pl.BlockSpec(memory_space=pltpu.VMEM)] * 2,
        out_specs=pl.BlockSpec(memory_space=pltpu.VMEM),
        scratch_shapes=[vmem((tiles, 3, 2, LANES), F32)],
        compiler_params=pltpu.CompilerParams(vmem_limit_bytes=60 * 2**20),
    )(landed, ctrl_place)


def solution(mesh):
    placed = (
        P(None, None, None, ("face", "tile")),
        P(None, None, ("face", "tile")),
        P("face", "tile", None),
        P("face", "tile", None),
        P("tile", "face"),
        P(),
        P(None, None, "tile", "face"),
        P(None, None, "tile", "face"),
        P("face", "tile", None),
        P("face", "tile", None),
    )
    return jax.shard_map(
        per_device,
        mesh=mesh,
        in_specs=placed,
        out_specs=P(None, None, None, ("face", "tile")),
        check_vma=False,
    )
```

```python
import functools

import jax
import jax.numpy as jnp
from jax import lax
from jax.experimental import pallas as pl
from jax.experimental.pallas import tpu as pltpu
from jax.sharding import PartitionSpec as P

MESH = pl.DeviceIdType.MESH
F32 = jnp.float32
BF16 = jnp.bfloat16
I32 = jnp.int32
I16 = jnp.int16

LEV = 90
STEPS = 5
LANES = 128
UNROLL = 10
CODE = 32000.0
SIDES = ((0, 1), (1, -1))


def ordered(slot, face0, face1):
    return (face0, face1) if slot % 2 == 0 else (face1, face0)


def stack_faces(slot, face0, face1):
    first, second = ordered(slot, face0, face1)
    return jnp.concatenate([first, second], axis=0)


def in_slot(index_array):
    rows = lax.broadcasted_iota(I32, (LANES, LANES), 0)
    return (rows == index_array).astype(F32)


def column_dot(lhs, rhs):
    return lax.dot_general(lhs, rhs, (((1,), (1,)), ((), ())), preferred_element_type=F32)


def row_dot(lhs, rhs):
    return lax.dot_general(lhs, rhs, (((0,), (1,)), ((), ())), preferred_element_type=F32)


def kernel(
    tiles,
    fwd, kap, send_order, recv_place, depth, rate_in, adj, mis, ctrl_send, ctrl_place,
    land_two,
    rate, fwd_v, kap_v, so_v, rp_v, depth_v, adj_v, mis_v, cs_v, cp_v,
    coup_v, stage, send_one, land_one,
    meta, metas, half_adj, half_mis, edge_adj, halo_adj, halo_mis, halo_edge, own_adj, own_mis,
    places, placed, give, take, state, middle, keep, factor, inverse, source,
    final, other, send_two, stage_pair,
    local, meta_sem, one_sem, pass_sem, halo_sem, pair_sem, two_sem,
):
    tile = lax.axis_index("tile")
    face = lax.axis_index("face")
    barrier = pltpu.get_barrier_semaphore()

    def to_tile(shift):
        return lax.rem(tile + (shift + tiles), tiles)

    def greet(step, carry):
        pl.semaphore_signal(
            barrier, inc=1, device_id=(face, lax.rem(tile + step, tiles)), device_id_type=MESH
        )
        return carry

    for shift in (-2, -1, 0, 1, 2):
        pl.semaphore_signal(
            barrier, inc=1, device_id=(1 - face, to_tile(shift)), device_id_type=MESH
        )
    lax.fori_loop(1, tiles, greet, 0)

    moves = [
        pltpu.make_async_copy(src, dst, local.at[i])
        for i, (src, dst) in enumerate((
            (fwd, fwd_v.at[:, pl.ds(0, LEV)]),
            (kap, kap_v.at[pl.ds(0, LEV)]),
            (send_order.at[0], so_v),
            (recv_place.at[0], rp_v),
            (depth, depth_v),
            (adj, adj_v),
            (mis, mis_v),
            (ctrl_send.at[0], cs_v),
            (ctrl_place.at[0], cp_v),
            (adj.at[face], own_adj.at[face]),
            (mis.at[face], own_mis.at[face]),
            (rate_in, rate),
        ))
    ]
    for move in moves:
        move.start()
    fwd_v[0, LEV] = jnp.zeros((4, LANES), BF16)
    fwd_v[1, LEV] = jnp.zeros((4, LANES), BF16)
    kap_v[LEV] = jnp.zeros((4, LANES), BF16)
    coup_v[pl.ds(4 * LEV, 24)] = jnp.zeros((24, LANES), F32)
    stage[:, 4, 1, :] = jnp.zeros((LANES, LANES), F32)

    for move in moves[:4]:
        move.wait()

    def density(level):
        return 0.8 * fwd_v[1, level].astype(F32) - 0.2 * fwd_v[0, level].astype(F32)

    def couple(block, carry):
        above, kappa_above = carry
        for pair in range(5):
            rows = []
            for half in range(2):
                level = block * 10 + pair * 2 + half + 1
                below = density(level)
                kappa_below = kap_v[level].astype(F32)
                contrast = below - above
                rows.append(
                    0.5 * (kappa_above + kappa_below) * (1.0 + 3.0 * jax.nn.sigmoid(-4.0 * contrast))
                )
                above, kappa_above = below, kappa_below
            coup_v[pl.ds(pl.multiple_of(block * 40 + pair * 8, 8), 8)] = jnp.concatenate(rows, axis=0)
        return above, kappa_above

    lax.fori_loop(0, LEV // 10, couple, (density(0), kap_v[0].astype(F32)))

    pick = in_slot(so_v[...]).T.astype(BF16)
    pieces = column_dot(pick, coup_v[...].astype(BF16))
    for beside in range(3):
        moved = pieces if beside == 1 else pltpu.roll(pieces, (1 - beside) % tiles, 0)
        for part in range(3):
            at = 3 * beside + part
            stage[:, at // 2, at % 2, :] = moved[:, part * LANES : (part + 1) * LANES]
    send_one[...] = stage[...].astype(BF16)

    moves[4].wait()
    meta[0] = jnp.concatenate([depth_v[...], depth_v[...]], axis=0)
    meta[1] = jnp.broadcast_to(rp_v[...], (8, LANES))
    metas[4 + face] = meta[...]
    moves[5].wait()
    for tracer in range(2):
        half_adj[tracer] = adj_v[tracer].astype(BF16)

    def outline(block, carry):
        for pair in range(3):
            level = 2 * (block * 3 + pair)
            for tracer in range(2):
                for side, line in ((0, 3), (1, 0)):
                    rows = [adj_v[tracer, level + half, line : line + 1, :] for half in range(2)]
                    edge_adj[side, tracer, block * 3 + pair] = jnp.concatenate(
                        rows, axis=0
                    ).astype(BF16)
        return carry

    lax.fori_loop(0, LEV // 6, outline, 0)
    moves[6].wait()
    for tracer in range(2):
        half_mis[tracer] = mis_v[tracer].astype(BF16)

    pl.semaphore_wait(barrier, tiles + 4)

    def remote(src, dst, send_sem, recv_sem, to_face, to):
        pltpu.make_async_remote_copy(
            src_ref=src, dst_ref=dst, send_sem=send_sem, recv_sem=recv_sem,
            device_id=(to_face, to), device_id_type=MESH,
        ).start()

    for shift in (-1, 1, -2, 2):
        for tracer in range(2):
            remote(
                meta, metas.at[2 * (2 - shift) + face],
                meta_sem.at[0], meta_sem.at[1], tracer, to_tile(shift),
            )
    remote(meta, metas.at[4 + face], meta_sem.at[0], meta_sem.at[1], 1 - face, tile)
    remote(
        adj.at[1 - face], own_adj.at[face], pair_sem.at[0], pair_sem.at[1], 1 - face, tile
    )
    remote(
        mis.at[1 - face], own_mis.at[face], pair_sem.at[2], pair_sem.at[3], 1 - face, tile
    )

    def route_one(step, carry):
        to = lax.rem(tile + step, tiles)
        remote(
            send_one.at[to], land_one.at[tile], one_sem.at[0], one_sem.at[1], face, to
        )
        return carry

    lax.fori_loop(1, tiles, route_one, 0)
    self_one = pltpu.make_async_copy(
        send_one.at[tile], land_one.at[tile], local.at[12]
    )
    self_one.start()
    for side, shift in SIDES:
        for tracer in range(2):
            remote(
                half_adj.at[tracer], halo_adj.at[2 * side + face],
                halo_sem.at[0], halo_sem.at[1], tracer, to_tile(shift),
            )
            remote(
                edge_adj.at[side, tracer], halo_edge.at[2 * side + face],
                halo_sem.at[2], halo_sem.at[3], tracer, to_tile(2 * shift),
            )
    for side, shift in SIDES:
        for tracer in range(2):
            remote(
                half_mis.at[tracer], halo_mis.at[2 * side + face],
                halo_sem.at[4], halo_sem.at[5], tracer, to_tile(shift),
            )

    def arrived(ref, semaphore):
        pltpu.make_async_copy(ref, ref, semaphore).wait()

    row = lax.broadcasted_iota(I32, (8, LANES), 0)
    lane = lax.broadcasted_iota(I32, (8, LANES), 1)
    cell = row % 4
    first_cell, last_cell = cell == 0, cell == 3
    first_lane, last_lane = lane == 0, lane == LANES - 1
    low_lane, low_row = lane < LANES // 2, row < 4
    east_wing = cell < 2
    seam_even = low_lane == low_row
    seam_odd = low_lane != low_row

    def neighbours(slot, west, here, east, to_west=None, to_east=None):
        to_west = here if to_west is None else to_west
        to_east = here if to_east is None else to_east
        seam = jnp.where(seam_even if slot % 2 == 0 else seam_odd, pltpu.roll(here, 4, 0), 0.0)
        return (
            pltpu.roll(jnp.where(first_cell, east, to_east), 7, 0),
            pltpu.roll(jnp.where(last_cell, west, to_west), 1, 0),
            pltpu.roll(jnp.where(first_lane, seam, here), LANES - 1, 1),
            pltpu.roll(jnp.where(last_lane, seam, here), 1, 1),
        )

    arrived(metas.at[pl.ds(0, 9)], meta_sem.at[1])
    depths = []
    for slot in range(5):
        at = tile + (slot - 2)
        inside = jnp.logical_and(at >= 0, at < tiles).astype(F32)
        first, second = ordered(slot, metas[2 * slot, 0], metas[2 * slot + 1, 0])
        depths.append(jnp.where(low_row, first, second).astype(F32) * inside)
    around = [
        neighbours(slot, depths[slot - 1], depths[slot], depths[slot + 1]) for slot in (1, 2, 3)
    ]

    def wet(level, slot):
        return level.astype(F32) < depths[slot]

    def store_wing(ref, level, values):
        for i in range(3):
            ref[level, i] = values[i]
        ref[level, 3] = jnp.where(east_wing, values[2], values[0])

    def prepare(block, carry):
        for inner in range(5):
            level = block * 5 + inner
            at = level.astype(F32)
            speed = rate[level]
            kept = []
            for slot in (1, 2, 3):
                count = jnp.zeros((8, LANES), F32)
                for beside in around[slot - 1]:
                    count = count + jnp.where(at < beside, 1.0, 0.0)
                kept.append(1.0 - speed * count)
            store_wing(keep, level, kept)
        return carry

    for part in range(3):
        places[part] = in_slot(metas[2 * (part + 1) + face, 1][0:1, :]).astype(BF16)
    moves[11].wait()
    lax.fori_loop(0, LEV // 5, prepare, 0)

    self_one.wait()
    arrived(land_one.at[pl.ds(0, tiles - 1)], one_sem.at[1])
    stage[...] = land_one[...].astype(F32)
    for part in range(3):
        held = jnp.concatenate(
            [stage[:, at // 2, at % 2, :] for at in range(3 * part, 3 * part + 3)], axis=1
        ).astype(BF16)
        result = row_dot(held, places[part])
        give[part] = result.astype(BF16)
        remote(
            give.at[part], take.at[part], pass_sem.at[part], pass_sem.at[3 + part], 1 - face, tile
        )
        placed[face, part] = result
    moves[9].wait()
    arrived(own_adj.at[0], pair_sem.at[1])
    arrived(halo_adj, halo_sem.at[1])
    arrived(halo_edge, halo_sem.at[3])

    def begin(block, carry):
        for inner in range(6):
            level = block * 6 + inner
            lines = [
                halo_edge[i, block * 3 + inner // 2].astype(F32)[inner % 2 : inner % 2 + 1]
                for i in range(4)
            ]
            tile_of = {
                1: stack_faces(1, halo_adj[0, level].astype(F32), halo_adj[1, level].astype(F32)),
                2: stack_faces(2, own_adj[0, level], own_adj[1, level]),
                3: stack_faces(3, halo_adj[2, level].astype(F32), halo_adj[3, level].astype(F32)),
                0: jnp.where(low_row, lines[0], lines[1]),
                4: jnp.where(low_row, lines[2], lines[3]),
            }
            for slot in range(5):
                state[level, slot] = jnp.where(wet(level, slot), tile_of[slot], 0.0)
        return carry

    lax.fori_loop(0, LEV // 6, begin, 0)
    for part in range(3):
        arrived(take.at[part], pass_sem.at[3 + part])
        placed[1 - face, part] = take[part].astype(F32)

    one = jnp.ones((8, LANES), F32)

    def eliminate(block, carry):
        carry = [(upper / lower, one) for upper, lower in carry]
        for pair in range(UNROLL // 2):
            base = pl.multiple_of(block * (4 * UNROLL) + pair * 8, 8)
            factors, inverses = ([], []), ([], [])
            for slot in (1, 2, 3):
                first, second = ordered(
                    slot, placed[0, slot - 1, pl.ds(base, 8)], placed[1, slot - 1, pl.ds(base, 8)]
                )
                couplings = (
                    jnp.where(low_row, first, pltpu.roll(second, 4, 0)),
                    jnp.where(low_row, pltpu.roll(first, 4, 0), second),
                )
                upper, lower = carry[slot - 1]
                for half in range(2):
                    level = block * UNROLL + pair * 2 + half
                    weight = jnp.where(
                        (level + 1).astype(F32) < depths[slot], couplings[half], 0.0
                    )
                    next_lower = upper + weight * lower
                    next_upper = next_lower + weight * upper
                    ratio = lower / next_lower
                    factors[half].append(weight * ratio)
                    inverses[half].append(jnp.where(wet(level, slot), ratio, 0.0))
                    upper, lower = next_upper, next_lower
                carry[slot - 1] = (upper, lower)
            for half in range(2):
                level = block * UNROLL + pair * 2 + half
                store_wing(factor, level, factors[half])
                store_wing(inverse, level, inverses[half])
        return carry

    lax.fori_loop(0, LEV // UNROLL, eliminate, [(one, one)] * 3)

    zero = jnp.zeros((8, LANES), F32)

    def across(slots, folding, level):
        held = {
            slot: state[level, slot]
            for slot in ((0, 1, 2, 3, 4) if 1 in slots else (1, 2, 3) if folding else (2, 5))
        }
        if 1 in slots:
            return [(held[slot], neighbours(slot, held[slot - 1], held[slot], held[slot + 1])) for slot in slots]
        here = held[2]
        if folding:
            west, east = held[1], held[3]
            wing = jnp.where(east_wing, east, west)
            to_east = jnp.where(last_cell, west, east)
            to_west = jnp.where(first_cell, east, west)
        else:
            west = east = wing = to_east = to_west = held[5]
        found = [(here, neighbours(2, west, here, east))]
        if 5 in slots:
            found.append((wing, neighbours(5, here, wing, here, to_west, to_east)))
        return found

    def descend(slots, folding=False):
        carry = [zero] * len(slots)
        for level in range(LEV):
            speed = rate[level]
            for i, (here, (east, west, north, south)) in enumerate(across(slots, folding, level)):
                at = slots[i] - 1 if slots[i] < 5 else 3
                value = (
                    keep[level, at] * here + speed * ((east + west) + (north + south)) + carry[i]
                )
                middle[level, at] = value
                carry[i] = factor[level, at] * value

    def swap(first, count, at):
        rows = pl.ds(first, count)
        remote(
            final.at[1 - face, rows], other.at[rows], pair_sem.at[at], pair_sem.at[at + 1], 1 - face, tile
        )

    def ascend(slots, last=False):
        carry = [zero] * len(slots)
        for pair in range(LEV // 2):
            halves = []
            for inner in range(2):
                level = LEV - 1 - (2 * pair + inner)
                for i, slot in enumerate(slots):
                    at = slot - 1 if slot < 5 else 3
                    solved = middle[level, at] * inverse[level, at] + factor[level, at] * carry[i]
                    carry[i] = solved
                    value = solved + source[level, at]
                    if last:
                        halves.append(value)
                    else:
                        state[level, slot] = value
            if last:
                below, above = halves
                base = 4 * LEV - 8 - 8 * pair
                final[0, pl.ds(base, 8)] = jnp.where(low_row, above, pltpu.roll(below, 4, 0))
                final[1, pl.ds(base, 8)] = jnp.where(low_row, pltpu.roll(above, 4, 0), below)
                if base == 176:
                    swap(176, 208, 6)

    descend((1, 2, 3))
    moves[10].wait()
    arrived(own_mis.at[0], pair_sem.at[3])
    arrived(halo_mis, halo_sem.at[5])

    def drive(block, carry):
        for inner in range(5):
            level = block * 5 + inner
            tile_of = {
                1: stack_faces(1, halo_mis[0, level].astype(F32), halo_mis[1, level].astype(F32)),
                2: stack_faces(2, own_mis[0, level], own_mis[1, level]),
                3: stack_faces(3, halo_mis[2, level].astype(F32), halo_mis[3, level].astype(F32)),
            }
            store_wing(
                source, level,
                [jnp.where(wet(level, slot), tile_of[slot], 0.0) for slot in (1, 2, 3)],
            )
        return carry

    lax.fori_loop(0, LEV // 5, drive, 0)

    ascend((1, 2, 3))
    descend((1, 2, 3))
    ascend((1, 2, 3))
    descend((2, 5), folding=True)
    ascend((2, 5))
    for step in range(3, STEPS - 1):
        descend((2, 5))
        ascend((2, 5))
    final[0, pl.ds(4 * LEV, 24)] = jnp.zeros((24, LANES), F32)
    final[1, pl.ds(4 * LEV, 24)] = jnp.zeros((24, LANES), F32)
    descend((2,))
    ascend((2,), last=True)

    swap(0, 176, 4)
    moves[7].wait()
    moves[8].wait()
    choose = in_slot(cs_v[...]).T.astype(BF16)
    end_lane = lax.broadcasted_iota(I32, (LANES, LANES), 1) == LANES - 1
    for source_of in range(2):
        if source_of == 0:
            values = final[face]
        else:
            arrived(other.at[pl.ds(0, 176)], pair_sem.at[5])
            arrived(other.at[pl.ds(176, 208)], pair_sem.at[7])
            values = other[...]
        high = values.astype(BF16)
        low = (values - high.astype(F32)).astype(BF16)
        pieces = column_dot(choose, high) + column_dot(choose, low)
        largest = jnp.max(jnp.abs(pieces), axis=1, keepdims=True)
        octave = jnp.ceil(4.0 * jnp.log2(jnp.maximum(largest, 1e-33)) + 0.01)
        codes = jnp.floor(pieces * (CODE / jnp.exp2(0.25 * octave)) + 0.5)
        for part in range(3):
            column = codes[:, part * LANES : (part + 1) * LANES]
            if part == 2:
                column = jnp.where(end_lane, octave, column)
            stage_pair[:, (3 * source_of + part) // 2, (3 * source_of + part) % 2, :] = column
    send_two[...] = stage_pair[...].astype(I32).astype(I16)

    def route_two(step, carry):
        to = lax.rem(tile + step, tiles)
        remote(send_two.at[to], land_two.at[tile], two_sem.at[0], two_sem.at[1], face, to)
        return carry

    lax.fori_loop(1, tiles, route_two, 0)
    self_two = pltpu.make_async_copy(send_two.at[tile], land_two.at[tile], local.at[13])
    self_two.start()
    self_two.wait()
    arrived(land_two.at[pl.ds(0, tiles - 1)], two_sem.at[1])

    arrived(metas.at[pl.ds(0, 9)], meta_sem.at[0])
    arrived(own_adj.at[0], pair_sem.at[0])
    arrived(own_mis.at[0], pair_sem.at[2])
    arrived(land_one.at[pl.ds(0, tiles - 1)], one_sem.at[0])
    arrived(halo_adj, halo_sem.at[0])
    arrived(halo_edge, halo_sem.at[2])
    arrived(halo_mis, halo_sem.at[4])
    for part in range(3):
        arrived(give.at[part], pass_sem.at[part])
    arrived(other.at[pl.ds(0, 176)], pair_sem.at[4])
    arrived(other.at[pl.ds(176, 208)], pair_sem.at[6])
    arrived(land_two.at[pl.ds(0, tiles - 1)], two_sem.at[0])


def deliver(land_two, cp_v, out, stage_pair):
    face = lax.axis_index("face")
    place = in_slot(cp_v[0]).astype(BF16)
    stage_pair[...] = land_two[...].astype(I32).astype(F32)
    for source_of in range(2):
        tracer = face if source_of == 0 else 1 - face
        values = jnp.concatenate(
            [stage_pair[:, part // 2, part % 2, :] for part in range(3 * source_of, 3 * source_of + 3)],
            axis=1,
        )
        octave = values[:, 3 * LANES - 1 :]
        values = values * (jnp.exp2(0.25 * octave) * (1.0 / CODE))
        high = values.astype(BF16)
        low = (values - high.astype(F32)).astype(BF16)
        result = row_dot(high, place) + row_dot(low, place)
        out[tracer] = result[: 4 * LEV].reshape(LEV, 4, LANES)


def per_device(
    fwd_tracers, fwd_kappa, send_order, recv_place, depth_levels, horiz_rate, adj_init, misfit,
    ctrl_send, ctrl_place,
):
    tiles = lax.axis_size("tile")
    anywhere = pl.BlockSpec(memory_space=pltpu.HBM)
    vmem = pltpu.VMEM
    dma = pltpu.SemaphoreType.DMA
    block = (LEV, 4, LANES)
    level_rows = (LEV, 4, 8, LANES)
    scratch = [
        pltpu.SMEM((LEV,), F32),
        vmem((2, LEV + 1, 4, LANES), BF16), vmem((LEV + 1, 4, LANES), BF16),
        vmem((1, LANES), I32), vmem((1, LANES), I32), vmem((4, LANES), I32),
        vmem((2,) + block, F32), vmem((2,) + block, F32),
        vmem((1, LANES), I32), vmem((1, LANES), I32),
        vmem((384, LANES), F32), vmem((tiles, 5, 2, LANES), F32),
        vmem((tiles, 5, 2, LANES), BF16), vmem((tiles, 5, 2, LANES), BF16),
        vmem((2, 8, LANES), I32), vmem((10, 2, 8, LANES), I32),
        vmem((2,) + block, BF16), vmem((2,) + block, BF16), vmem((2, 2, LEV // 2, 2, LANES), BF16),
        vmem((4,) + block, BF16), vmem((4,) + block, BF16), vmem((4, LEV // 2, 2, LANES), BF16),
        vmem((2,) + block, F32), vmem((2,) + block, F32),
        vmem((3, LANES, LANES), BF16),
        vmem((2, 3, 384, LANES), F32), vmem((3, 384, LANES), BF16), vmem((3, 384, LANES), BF16),
        vmem((LEV, 6, 8, LANES), F32),
        vmem(level_rows, F32), vmem(level_rows, F32), vmem(level_rows, F32),
        vmem(level_rows, F32), vmem(level_rows, F32),
        vmem((2, 384, LANES), F32), vmem((384, LANES), F32),
        vmem((tiles, 3, 2, LANES), I16),
        vmem((tiles, 3, 2, LANES), F32),
        dma((14,)), dma((2,)), dma((2,)), dma((6,)), dma((6,)), dma((8,)), dma((2,)),
    ]
    landed = pl.pallas_call(
        functools.partial(kernel, tiles),
        out_shape=jax.ShapeDtypeStruct((tiles, 3, 2, LANES), I16),
        in_specs=[anywhere] * 10,
        out_specs=pl.BlockSpec(memory_space=pl.ANY),
        scratch_shapes=scratch,
        compiler_params=pltpu.CompilerParams(
            collective_id=0, has_side_effects=True, vmem_limit_bytes=60 * 2**20
        ),
        cost_estimate=pl.CostEstimate(
            flops=10**9, bytes_accessed=4 * 2**20, transcendentals=10**5
        ),
    )(
        fwd_tracers, fwd_kappa, send_order, recv_place, depth_levels, horiz_rate, adj_init, misfit,
        ctrl_send, ctrl_place,
    )
    return pl.pallas_call(
        deliver,
        out_shape=jax.ShapeDtypeStruct((2,) + block, F32),
        in_specs=[pl.BlockSpec(memory_space=pltpu.VMEM)] * 2,
        out_specs=pl.BlockSpec(memory_space=pltpu.VMEM),
        scratch_shapes=[vmem((tiles, 3, 2, LANES), F32)],
        compiler_params=pltpu.CompilerParams(vmem_limit_bytes=60 * 2**20),
    )(landed, ctrl_place)


def solution(mesh):
    placed = (
        P(None, None, None, ("face", "tile")),
        P(None, None, ("face", "tile")),
        P("face", "tile", None),
        P("face", "tile", None),
        P("tile", "face"),
        P(),
        P(None, None, "tile", "face"),
        P(None, None, "tile", "face"),
        P("face", "tile", None),
        P("face", "tile", None),
    )
    return jax.shard_map(
        per_device,
        mesh=mesh,
        in_specs=placed,
        out_specs=P(None, None, None, ("face", "tile")),
        check_vma=False,
    )
```
